128 devices in a mesh: dom: 16 (over z, y_lo, core), bead: 8 (over y_hi, x).
Axes of the slice: x: 4, y: 4 (y_hi: 2, y_lo: 2; y = y_hi * 2 + y_lo), z: 4, core: 2. Of those that a mesh axis runs over, the one named last changes fastest.
Arguments:
- positions: float32 [8, 3, 8192], P('bead', None, 'dom'), may hold values from -6 to 6
- velocities: float32 [8, 3, 8192], P('bead', None, 'dom'), may hold values from -6 to 6
- species: int32 [8192], P('dom'), may hold values from 0 to 1
- neighbours: int32 [32, 8192], P(None, 'dom'), may hold values from 0 to 767
- neighbour_count: int32 [8192], P('dom'), may hold values from 16 to 32, as said below
- send_lists: int32 [2, 2048], P(None, 'dom'), may hold values from 0 to 511
- projection: float32 [2, 3, 512], replicated, may hold values from -4 to 4
- phase_shift: float32 [2, 512], replicated, may hold values from -3.140625 to 3.140625
- points: bfloat16 [2, 2000, 512], P(None, 'bead'), may hold values from -0.25 to 0.25
- point_weights: bfloat16 [2, 2000], P(None, 'bead'), may hold values from -0.125 to 0.125
Outputs:
- new_positions: float32 [8, 3, 8192], P('bead', None, 'dom')
- new_velocities: float32 [8, 3, 8192], P('bead', None, 'dom')
The draws below stay inside these ranges and needn't reach their ends.
Inputs may be any that keep to these rules, and one draw needn't show every extreme that they name: `neighbours`: slots below 512 are atoms of the domain itself, the next 128 the atoms received from the domain below, the last 128 those from the domain above; domains form a closed loop; entries past an atom's count are padding. `neighbour_count`: every domain has an atom with all 32 slots valid. `send_lists`: local atom numbers of the sending domain; an atom may be listed more than once.
All inputs are finite; a program needn't handle non-finite values.
Results may differ from the reference program's by a relative error of at most 0.019.
Values may be sent and summed in bfloat16 or wider, within the bound.
No kernel may reach another device: no remote copies, remote signals or barrier semaphores. Data moves between devices by JAX's collectives and lax.ppermute only.
A program may use at most 128 MiB of HBM per device.

```python
import jax
import jax.numpy as jnp
from jax import lax

SOAP = 512
POINTS = 2000
ATOM_DEV = 512
NEIGH = 32
GHOSTS = 128
STEPS = 2
ATOMS = 8192
BEADS = 8
GHOST_ALL = 2048
N_DOM = 16


def draw_neighbour_count(key, part):
    key = jax.random.fold_in(key, 11)
    counts = jax.random.randint(key, (ATOMS,), NEIGH // 2, NEIGH + 1)
    return counts.at[::ATOM_DEV].set(NEIGH).astype(jnp.int32)


def touch_ends(result, key, smallest, top_value):
    longest = result.shape.index(max(result.shape))
    spots = []
    for shift in (0, 1):
        where = [jax.random.randint(jax.random.fold_in(key, axis), (), 0, length) for axis, length in enumerate(result.shape)]
        where[longest] = (where[longest] + shift) % result.shape[longest]
        spots.append(tuple(where))
    return result.at[spots[0]].set(smallest).at[spots[1]].set(top_value)


def level_of(stream_key, extent, cuts, smallest, high):
    def one(dim, shards_of):
        heights = jax.random.uniform(jax.random.fold_in(jax.random.fold_in(stream_key, 6), dim), (shards_of,), jnp.float32, smallest / len(cuts), high / len(cuts))
        return jnp.repeat(jnp.exp(heights), extent[dim] // shards_of).reshape((-1,) + (1,) * (len(extent) - dim - 1))

    factor_of = one(*cuts[0])
    for cut in cuts[1:]:
        factor_of = factor_of * one(*cut)
    return factor_of


def bell_draw(stream_key, extent, deviation, reach, cuts=(), held_as=jnp.bfloat16):
    entries = jax.random.normal(stream_key, extent, jnp.float32) * deviation
    if len(cuts) > 0:
        entries = level_of(stream_key, extent, cuts, -0.22, 0.18) * entries
    return jnp.clip(entries, min=-reach, max=reach).astype(held_as)


def setup_inputs(seed: int = 0) -> dict:
    key_list = jax.random.split(jax.random.key(seed), 11)
    return {
        "positions": bell_draw(key_list[0], (BEADS, 3, ATOMS), 1.0, 6.0, ((0, 8), (2, 16)), jnp.float32),
        "velocities": bell_draw(key_list[1], (BEADS, 3, ATOMS), 1.0, 6.0, ((0, 8), (2, 16)), jnp.float32),
        "species": touch_ends(jax.random.randint(key_list[2], (ATOMS,), 0, 2), jax.random.fold_in(key_list[2], 1), 0, 1).astype(jnp.int32),
        "neighbours": touch_ends(jax.random.randint(key_list[3], (NEIGH, ATOMS), 0, ATOM_DEV + 2 * GHOSTS), jax.random.fold_in(key_list[3], 1), 0, (ATOM_DEV + 2 * GHOSTS) - 1).astype(jnp.int32),
        "neighbour_count": draw_neighbour_count(jax.random.fold_in(key_list[10], 71), 0),
        "send_lists": touch_ends(jax.random.randint(key_list[5], (2, GHOST_ALL), 0, ATOM_DEV), jax.random.fold_in(key_list[5], 1), 0, ATOM_DEV - 1).astype(jnp.int32),
        "projection": bell_draw(key_list[6], (2, 3, SOAP), 1.0, 4.0, (), jnp.float32),
        "phase_shift": jnp.clip(jax.random.uniform(key_list[7], (2, SOAP), jnp.float32, -3.140625, 3.140625), -3.140625, 3.140625),
        "points": bell_draw(key_list[8], (2, POINTS, SOAP), SOAP ** -0.5, 0.25, ((1, 8),)),
        "point_weights": bell_draw(key_list[9], (2, POINTS), POINTS ** -0.5, 0.125, ((1, 8),)),
    }


WIDTH = 1.5
DT = 0.1
KAPPA = 0.5
SLOT_BLOCK = 8


def global_lists(neighbours, send_lists):
    sends = send_lists.reshape(2, N_DOM, GHOSTS)
    domains = jnp.arange(N_DOM, dtype=jnp.int32)
    lower = (domains - 1) % N_DOM
    upper = (domains + 1) % N_DOM
    own = domains[:, None] * ATOM_DEV + jnp.arange(ATOM_DEV, dtype=jnp.int32)[None, :]
    from_lower = lower[:, None] * ATOM_DEV + sends[1][lower]
    from_upper = upper[:, None] * ATOM_DEV + sends[0][upper]
    table = jnp.concatenate([own, from_lower, from_upper], axis=1).astype(jnp.int32)
    local = neighbours.reshape(NEIGH, N_DOM, ATOM_DEV)
    wide = jnp.broadcast_to(table[None], (NEIGH,) + table.shape)
    return jnp.take_along_axis(wide, local, axis=2).reshape(NEIGH, ATOMS).astype(jnp.int32)


def pair_geometry(position, near, species_near, valid, projection, phase_shift):
    offset = near - position[:, None, :]
    weight = valid * jnp.exp(-(offset[0] ** 2 + offset[1] ** 2 + offset[2] ** 2) / (2.0 * WIDTH * WIDTH))
    change = projection[1] - projection[0]
    phase = phase_shift[0][None, :, None] + species_near[:, None, :] * (phase_shift[1] - phase_shift[0])[None, :, None]
    coeffs = []
    for axis_id in range(3):
        coeff = projection[0][axis_id][None, :, None] + species_near[:, None, :] * change[axis_id][None, :, None]
        phase = phase + coeff * offset[axis_id][:, None, :]
        coeffs.append(coeff)
    return offset, weight, phase, coeffs


def potential_force(position, species, species_value, glob, neighbour_count, projection, phase_shift, flat_points, scale):
    slots = jnp.arange(NEIGH, dtype=jnp.int32)
    descriptor = jnp.zeros((SOAP, ATOMS), jnp.float32)
    for start in range(0, NEIGH, SLOT_BLOCK):
        index = glob[start:start + SLOT_BLOCK]
        valid = (slots[start:start + SLOT_BLOCK][:, None] < neighbour_count[None, :]).astype(jnp.float32)
        offset, weight, phase, coeffs = pair_geometry(position, position[:, index], species_value[index], valid, projection, phase_shift)
        descriptor = descriptor + jnp.sum(weight[:, None, :] * jnp.cos(phase), axis=0)
    q_low = descriptor.astype(jnp.bfloat16)
    u = jnp.dot(flat_points.astype(jnp.float32), q_low.astype(jnp.float32), preferred_element_type=jnp.float32)
    row_species = jnp.arange(2 * POINTS, dtype=jnp.int32) // POINTS
    coefficient = jnp.where(row_species[:, None] == species[None, :], scale[:, None] * u, 0.0).astype(jnp.bfloat16)
    gradient = lax.dot_general(flat_points.astype(jnp.float32), coefficient.astype(jnp.float32), (((0,), (0,)), ((), ())), preferred_element_type=jnp.float32)
    force = jnp.zeros((3, ATOMS), jnp.float32)
    for start in range(0, NEIGH, SLOT_BLOCK):
        index = glob[start:start + SLOT_BLOCK]
        valid = (slots[start:start + SLOT_BLOCK][:, None] < neighbour_count[None, :]).astype(jnp.float32)
        offset, weight, phase, coeffs = pair_geometry(position, position[:, index], species_value[index], valid, projection, phase_shift)
        with_sin = gradient[None] * jnp.sin(phase)
        along = jnp.sum(gradient[None] * jnp.cos(phase), axis=1)
        terms = jnp.stack([-weight * (jnp.sum(with_sin * coeffs[a], axis=1) + along * offset[a] / (WIDTH * WIDTH)) for a in range(3)])
        force = force + jnp.sum(terms, axis=1)
        force = force.at[:, index].add(-terms)
    return force


def reference(positions, velocities, species, neighbours, neighbour_count, send_lists, projection, phase_shift, points, point_weights):
    glob = global_lists(neighbours, send_lists)
    species_value = species.astype(jnp.float32)
    mass = jnp.where(species == 0, 16.0, 1.0).astype(jnp.float32)
    flat_points = points.reshape(2 * POINTS, SOAP)
    scale = 2.0 * point_weights.reshape(2 * POINTS).astype(jnp.float32)
    place = positions
    speed = velocities
    for step in range(STEPS):
        pot = lax.map(lambda bead_pos: potential_force(bead_pos, species, species_value, glob, neighbour_count, projection, phase_shift, flat_points, scale), place)
        chain = 2.0 * place - jnp.roll(place, 1, axis=0) - jnp.roll(place, -1, axis=0)
        total = pot - KAPPA * mass * chain
        speed = speed + DT * (total / mass)
        place = place + DT * speed
    return place, speed
```

```python
import functools

import jax
import jax.numpy as jnp
from jax import lax
from jax.experimental import pallas as pl
from jax.experimental.pallas import tpu as pltpu
from jax.sharding import PartitionSpec as P

NEIGH = 32
STEPS = 2

WIDTH = 1.5
DT = 0.1
KAPPA = 0.5

F32, BF16 = jnp.float32, jnp.bfloat16
LANES = 128
ROWS = 16
FB = 256
TURN = 0.15915494309189535
SIN = (3.1415927410125732, -5.167710304260254, 2.550077438354492, -0.5982903838157654, 0.07765591144561768)
COS = (0.9999999403953552, -4.934792995452881, 4.05841064453125, -1.3318729400634766, 0.21968242526054382)
VMEM = pl.BlockSpec(memory_space=pltpu.VMEM)
PARAMS = pltpu.CompilerParams(vmem_limit_bytes=60 * 1024 * 1024)


def call(body, outs, scratch=()):
    return pl.pallas_call(
        body,
        out_shape=outs,
        out_specs=jax.tree.map(lambda _: VMEM, outs),
        scratch_shapes=scratch,
        compiler_params=PARAMS,
    )


def cos_sin(turns):
    f = turns - jnp.round(turns)
    g = f * f
    s, c = SIN[-1], COS[-1]
    for low in SIN[-2::-1]:
        s = s * g + low
    for low in COS[-2::-1]:
        c = c * g + low
    s = s * f
    twice = s + s
    return 1.0 - twice * s, twice * c


def count_kernel(neighbours_ref, count_ref, number_ref, named):
    slot = lax.broadcasted_iota(jnp.int32, neighbours_ref.shape, 0)
    named[...] = jnp.where(slot < count_ref[...], neighbours_ref[...], -1)
    rows = 32
    atoms = neighbours_ref.shape[1]

    def chunk(c, carry):
        first = pl.multiple_of(c * rows, rows)
        local = lax.broadcasted_iota(jnp.int32, (rows, atoms), 0) + first
        total = jnp.zeros((rows, atoms), F32)
        for k in range(NEIGH):
            total = total + jnp.where(local == named[k : k + 1, :], 1.0, 0.0)
        number_ref[pl.ds(first, rows), :] = total
        return carry

    lax.fori_loop(0, number_ref.shape[0] // rows, chunk, 0)


def gather_rows(columns, list_row, count):
    atoms, listed = columns.shape[0], list_row.shape[1]
    hit = lax.broadcasted_iota(jnp.int32, (atoms, listed), 0) == list_row
    return [
        jnp.sum(jnp.where(hit, columns[:, a : a + 1], 0.0), axis=0, keepdims=True)
        for a in range(count)
    ]


def send_rows(position_rows, species_row, lists_ref, down_ref, up_ref, wide):
    wide[...] = jnp.zeros_like(wide)
    for a in range(3):
        wide[a : a + 1, :] = position_rows[a]
    wide[3:4, :] = species_row
    columns = wide[...].T
    for out, which in ((down_ref, 0), (up_ref, 1)):
        for a, row in enumerate(gather_rows(columns, lists_ref[which : which + 1, :], 4)):
            out[a : a + 1, :] = row


def first_kernel(position_ref, species_ref, lists_ref, down_ref, up_ref, wide):
    rows = [position_ref[0, a : a + 1, :] for a in range(3)]
    send_rows(rows, species_ref[...].astype(F32), lists_ref, down_ref, up_ref, wide)


def update_kernel(
    last,
    force_ref,
    back_lower_ref,
    back_upper_ref,
    lists_ref,
    position_ref,
    velocity_ref,
    before_ref,
    after_ref,
    species_ref,
    new_position_ref,
    new_velocity_ref,
    *rest,
):
    atoms = position_ref.shape[2]
    listed = lists_ref.shape[1]
    wide = rest[-1]
    extra = [0.0, 0.0, 0.0]
    back = rest[-2]
    for which, ref in ((0, back_lower_ref), (1, back_upper_ref)):
        back[...] = jnp.zeros_like(back)
        back[0:3, :] = ref[...]
        values = back[...].T
        back[0:1, :] = lists_ref[which : which + 1, :].astype(F32)
        names = back[...].T[:, 0:1]
        hit = lax.broadcasted_iota(jnp.int32, (listed, atoms), 1).astype(F32) == names
        for a in range(3):
            extra[a] = extra[a] + jnp.sum(
                jnp.where(hit, values[:, a : a + 1], 0.0), axis=0, keepdims=True
            )
    species = species_ref[...]
    mass = jnp.where(species == 0, 16.0, 1.0)
    rows = []
    for a in range(3):
        here = position_ref[0, a : a + 1, :]
        chain = 2.0 * here - before_ref[0, a : a + 1, :] - after_ref[0, a : a + 1, :]
        total = force_ref[a : a + 1, 0:atoms] + extra[a] - KAPPA * mass * chain
        velocity = velocity_ref[0, a : a + 1, :] + DT * (total / mass)
        place = here + DT * velocity
        new_velocity_ref[0, a : a + 1, :] = velocity
        new_position_ref[0, a : a + 1, :] = place
        rows.append(place)
    if not last:
        send_rows(rows, species.astype(F32), lists_ref, rest[0], rest[1], wide)


def force_kernel(
    position_ref,
    species_ref,
    lower_ref,
    upper_ref,
    number_ref,
    projection_ref,
    shift_ref,
    matrix_ref,
    force_ref,
    near,
    cols,
    weight,
    weight_low,
    weight_turned,
    waves,
    turned,
    sums,
    sines,
    low,
    grad,
    spread,
    product,
    back,
    parts,
):
    own = position_ref.shape[2]
    ghosts = lower_ref.shape[1]
    everyone = own + 2 * ghosts
    features = projection_ref.shape[2]
    blocks = features // FB

    near[...] = jnp.zeros_like(near)
    near[0:3, 0:own] = position_ref[0]
    near[3:4, 0:own] = species_ref[...].astype(F32)
    near[0:4, own : own + ghosts] = lower_ref[...]
    near[0:4, own + ghosts : everyone] = upper_ref[...]
    cols[...] = near[...].T

    here = [near[a : a + 1, 0:own] for a in range(3)]

    def weigh(c, carry):
        rows = pl.ds(pl.multiple_of(c * ROWS, ROWS), ROWS)
        there = cols[rows, :]
        square = 0.0
        for a in range(3):
            d = there[:, a : a + 1] - here[a]
            square = square + d * d
        w = number_ref[rows, :] * jnp.exp(square * (-1.0 / (2.0 * WIDTH * WIDTH)))
        weight[rows, :] = w
        weight_low[rows, :] = w.astype(BF16)
        return carry

    lax.fori_loop(0, everyone // ROWS, weigh, 0, unroll=2)
    weight_turned[...] = weight[...].T.astype(BF16)

    shift_cos, shift_sin = cos_sin(shift_ref[...] * TURN)

    for block in range(blocks):
        mine = slice(block * FB, (block + 1) * FB)
        base = block * 4 * FB
        wave = [
            [projection_ref[s, a : a + 1, mine] * TURN for a in range(3)] for s in range(2)
        ]
        turn_cos = [shift_cos[s : s + 1, mine] for s in range(2)]
        turn_sin = [shift_sin[s : s + 1, mine] for s in range(2)]

        def own_waves(c, carry):
            rows = pl.ds(pl.multiple_of(c * ROWS, ROWS), ROWS)
            there = cols[rows, :]
            x, y, z = (jnp.broadcast_to(there[:, a : a + 1], (ROWS, FB)) for a in range(3))
            second = jnp.broadcast_to(there[:, 3:4], (ROWS, FB)) > 0.5
            for s in range(2):
                cos, sin = cos_sin(x * wave[s][0] + y * wave[s][1] + z * wave[s][2])
                at = base + s * 2 * FB
                turned[rows, at : at + FB] = turn_cos[s] * cos + turn_sin[s] * sin
                turned[rows, at + FB : at + 2 * FB] = turn_sin[s] * cos - turn_cos[s] * sin
                if s == 0:
                    cos, sin = jnp.where(second, 0.0, cos), jnp.where(second, 0.0, sin)
                else:
                    cos, sin = jnp.where(second, cos, 0.0), jnp.where(second, sin, 0.0)
                waves[rows, at : at + FB] = cos.astype(BF16)
                waves[rows, at + FB : at + 2 * FB] = sin.astype(BF16)
            return carry

        lax.fori_loop(0, own // ROWS, own_waves, 0)

        def ghost_waves(c, carry):
            rows = pl.ds(pl.multiple_of(own + c * ROWS, ROWS), ROWS)
            there = cols[rows, :]
            x, y, z = (jnp.broadcast_to(there[:, a : a + 1], (ROWS, FB)) for a in range(3))
            second = jnp.broadcast_to(there[:, 3:4], (ROWS, FB)) > 0.5
            px, py, pz = (jnp.where(second, wave[1][a], wave[0][a]) for a in range(3))
            cos, sin = cos_sin(x * px + y * py + z * pz)
            for s in range(2):
                at = base + s * 2 * FB
                for k, part in enumerate((cos, sin)):
                    if s == 0:
                        part = jnp.where(second, 0.0, part)
                    else:
                        part = jnp.where(second, part, 0.0)
                    waves[rows, at + k * FB : at + (k + 1) * FB] = part.astype(BF16)
            return carry

        lax.fori_loop(0, 2 * ghosts // ROWS, ghost_waves, 0)

        sums[...] = jnp.dot(
            weight_turned[...], waves[:, base : base + 4 * FB], preferred_element_type=F32
        )

        def describe(c, carry):
            rows = pl.ds(pl.multiple_of(c * ROWS, ROWS), ROWS)
            total = 0.0
            for s in range(2):
                at = base + s * 2 * FB
                tr, ti = turned[rows, at : at + FB], turned[rows, at + FB : at + 2 * FB]
                ur = sums[rows, s * 2 * FB : s * 2 * FB + FB]
                ui = sums[rows, s * 2 * FB + FB : s * 2 * FB + 2 * FB]
                total = total + (tr * ur - ti * ui)
                first = s * features + block * FB
                sines[rows, first : first + FB] = tr * ui + ti * ur
            low[rows, mine] = total.astype(BF16)
            return carry

        lax.fori_loop(0, own // ROWS, describe, 0)

    species = cols[0:own, 3:4]
    grad[...] = jnp.where(
        species > 0.5,
        jnp.dot(low[...], matrix_ref[features : 2 * features, :], preferred_element_type=F32),
        jnp.dot(low[...], matrix_ref[0:features, :], preferred_element_type=F32),
    )

    parts[...] = jnp.zeros_like(parts)

    def fold(value):
        total = value[:, 0:LANES]
        for k in range(1, value.shape[1] // LANES):
            total = total + value[:, k * LANES : (k + 1) * LANES]
        return total

    for block in range(blocks):
        mine = slice(block * FB, (block + 1) * FB)
        base = block * 4 * FB
        raw = [[projection_ref[s, a : a + 1, mine] for a in range(3)] for s in range(2)]

        def spread_out(c, carry):
            rows = pl.ds(pl.multiple_of(c * ROWS, ROWS), ROWS)
            g = grad[rows, mine]
            first = block * FB
            t0 = g * sines[rows, first : first + FB]
            t1 = g * sines[rows, features + first : features + first + FB]
            for a in range(3):
                parts[a, rows, :] = parts[a, rows, :] - fold(t0 * raw[0][a] + t1 * raw[1][a])
            for s in range(2):
                at = base + s * 2 * FB
                spread[rows, at : at + FB] = (g * turned[rows, at : at + FB]).astype(BF16)
                spread[rows, at + FB : at + 2 * FB] = (
                    -g * turned[rows, at + FB : at + 2 * FB]
                ).astype(BF16)
            return carry

        lax.fori_loop(0, own // ROWS, spread_out, 0)
        back[...] = jnp.dot(
            weight_low[...], spread[:, base : base + 4 * FB], preferred_element_type=F32
        )

        def pull(c, carry):
            rows = pl.ds(pl.multiple_of(c * ROWS, ROWS), ROWS)
            second = jnp.broadcast_to(cols[rows, 3:4], (ROWS, FB)) > 0.5
            total = 0.0
            for s in range(2):
                at = base + s * 2 * FB
                er = waves[rows, at : at + FB].astype(F32)
                ei = waves[rows, at + FB : at + 2 * FB].astype(F32)
                vr = back[rows, s * 2 * FB : s * 2 * FB + FB]
                vi = back[rows, s * 2 * FB + FB : s * 2 * FB + 2 * FB]
                total = total + (ei * vr - er * vi)
            for a in range(3):
                coeff = jnp.where(second, raw[1][a], raw[0][a])
                parts[a, rows, :] = parts[a, rows, :] + fold(total * coeff)
            return carry

        lax.fori_loop(0, everyone // ROWS, pull, 0)

    product[...] = lax.dot_general(
        waves[...], spread[...], (((1,), (1,)), ((), ())), preferred_element_type=F32
    )

    def along(c, carry):
        rows = pl.ds(pl.multiple_of(c * ROWS, ROWS), ROWS)
        there = cols[rows, :]
        z = weight[rows, :] * product[rows, :] * (1.0 / (WIDTH * WIDTH))
        out = []
        for a in range(3):
            pull_a = z * (there[:, a : a + 1] - here[a])
            parts[a, rows, :] = parts[a, rows, :] + fold(pull_a)
            total = pull_a[0:8]
            for k in range(1, ROWS // 8):
                total = total + pull_a[8 * k : 8 * k + 8]
            out.append(carry[a] + total)
        return tuple(out)

    centre = lax.fori_loop(
        0,
        everyone // ROWS,
        along,
        tuple(jnp.zeros((8, own), F32) for _ in range(3)),
    )
    for a in range(3):
        row = jnp.sum(parts[a].T, axis=0, keepdims=True)
        force_ref[a : a + 1, 0:own] = row[:, 0:own] - jnp.sum(centre[a], axis=0, keepdims=True)
        force_ref[a : a + 1, own:everyone] = row[:, own:everyone]


def passed_along(block, axis, distance):
    devices = range(lax.axis_size(axis))
    route = [((i - distance) % len(devices), i) for i in devices]
    return lax.ppermute(block, axis, route)


def routed(block, axis, source):
    return lax.ppermute(block, axis, [(source(i), i) for i in range(lax.axis_size(axis))])


def kernel_matrix(points, point_weights):
    features = points.shape[2]
    dom, bead = lax.axis_index("dom"), lax.axis_index("bead")
    place = dom % 2 * 8 + dom // 4 * 2 + dom // 2 % 2
    which, height = place // 8, features // 8
    p = lax.dynamic_index_in_dim(points, which, 0, keepdims=False).astype(F32)
    w = lax.dynamic_index_in_dim(point_weights, which, 0, keepdims=False).astype(F32)
    left = lax.dynamic_slice_in_dim(p, place % 8 * height, height, axis=1)
    part = lax.dot_general(
        left * (2.0 * w)[:, None],
        p,
        (((0,), (0,)), ((), ())),
        precision=lax.Precision.HIGHEST,
        preferred_element_type=F32,
    )
    other = routed(part.astype(BF16), "bead", lambda i: i ^ 4)
    part = part + other.astype(F32)
    sent = part.astype(BF16)
    for k in (1, 2, 3):
        part = part + routed(sent, "bead", lambda i: i // 4 * 4 + (i - k) % 4).astype(F32)
    held = part.astype(BF16)
    other = routed(held, "dom", lambda i: i ^ 2)
    upper = dom // 2 % 2 == 1
    held = jnp.where(upper, jnp.concatenate([other, held]), jnp.concatenate([held, other]))
    rows = held.shape[0]
    pieces = [routed(held, "dom", lambda i: (i - 4 * k) % 16) for k in (3, 2, 1)] + [held]
    held = lax.dynamic_slice_in_dim(
        jnp.concatenate(pieces + pieces), (3 - dom // 4) % 4 * rows, 4 * rows, axis=0
    )
    other = routed(held, "dom", lambda i: i ^ 1)
    return jnp.where(
        dom % 2 == 1, jnp.concatenate([other, held]), jnp.concatenate([held, other])
    )


def shards(
    positions,
    velocities,
    species,
    neighbours,
    neighbour_count,
    send_lists,
    projection,
    phase_shift,
    points,
    point_weights,
):
    own, ghosts = positions.shape[2], send_lists.shape[1]
    everyone = own + 2 * ghosts
    features = points.shape[2]
    shape = jax.ShapeDtypeStruct
    species = species.reshape(1, own)
    sent = (shape((4, ghosts), F32),) * 2
    wide = pltpu.VMEM((LANES, own), F32)

    going_down, going_up = call(first_kernel, sent, [wide])(positions, species, send_lists)
    number = call(
        count_kernel, shape((everyone, own), F32), [pltpu.VMEM((NEIGH, own), jnp.int32)]
    )(neighbours, neighbour_count.reshape(1, own))
    matrix = kernel_matrix(points, point_weights)

    force_call = call(
        force_kernel,
        shape((3, everyone), F32),
        [
            pltpu.VMEM((LANES, everyone), F32),
            pltpu.VMEM((everyone, LANES), F32),
            pltpu.VMEM((everyone, own), F32),
            pltpu.VMEM((everyone, own), BF16),
            pltpu.VMEM((own, everyone), BF16),
            pltpu.VMEM((everyone, 4 * features), BF16),
            pltpu.VMEM((own, 4 * features), F32),
            pltpu.VMEM((own, 4 * FB), F32),
            pltpu.VMEM((own, 2 * features), F32),
            pltpu.VMEM((own, features), BF16),
            pltpu.VMEM((own, features), F32),
            pltpu.VMEM((own, 4 * features), BF16),
            pltpu.VMEM((everyone, own), F32),
            pltpu.VMEM((everyone, 4 * FB), F32),
            pltpu.VMEM((3, everyone, LANES), F32),
        ],
    )
    for step in range(STEPS):
        from_lower = passed_along(going_up, "dom", 1)
        from_upper = passed_along(going_down, "dom", -1)
        before = passed_along(positions, "bead", 1)
        after = passed_along(positions, "bead", -1)
        force = force_call(
            positions, species, from_lower, from_upper, number, projection, phase_shift, matrix
        )
        back_from_lower = passed_along(force[:, own + ghosts :], "dom", 1)
        back_from_upper = passed_along(force[:, own : own + ghosts], "dom", -1)
        last = step == STEPS - 1
        moved = shape(positions.shape, F32)
        positions, velocities, *sends = call(
            functools.partial(update_kernel, last),
            (moved, moved) + (() if last else sent),
            [pltpu.VMEM((LANES, ghosts), F32), wide],
        )(
            force,
            back_from_lower,
            back_from_upper,
            send_lists,
            positions,
            velocities,
            before,
            after,
            species,
        )
        if not last:
            going_down, going_up = sends
    return (positions, velocities)


def solution(mesh):
    placed = (
        P("bead", None, "dom"),
        P("bead", None, "dom"),
        P("dom"),
        P(None, "dom"),
        P("dom"),
        P(None, "dom"),
        P(),
        P(),
        P(None, "bead", None),
        P(None, "bead"),
    )
    return jax.shard_map(
        shards,
        mesh=mesh,
        in_specs=placed,
        out_specs=(P("bead", None, "dom"), P("bead", None, "dom")),
        check_vma=False,
    )
```

```python
import functools

import jax
import jax.numpy as jnp
from jax import lax
from jax.experimental import pallas as pl
from jax.experimental.pallas import tpu as pltpu
from jax.sharding import PartitionSpec as P

NEIGH = 32
STEPS = 2

WIDTH = 1.5
DT = 0.1
KAPPA = 0.5

F32, BF16 = jnp.float32, jnp.bfloat16
LANES = 128
ROWS = 32
FB = 256
TURN = 0.15915494309189535
SIN = (3.1415927410125732, -5.167710304260254, 2.550077438354492, -0.5982903838157654, 0.07765591144561768)
COS = (0.9999999403953552, -4.934792995452881, 4.05841064453125, -1.3318729400634766, 0.21968242526054382)
VMEM = pl.BlockSpec(memory_space=pltpu.VMEM)
MIB = 1024 * 1024
LIMIT = 16


def call(body, outs, scratch=(), limit=8):
    return pl.pallas_call(
        body,
        out_shape=outs,
        out_specs=jax.tree.map(lambda _: VMEM, outs),
        scratch_shapes=scratch,
        compiler_params=pltpu.CompilerParams(vmem_limit_bytes=limit * MIB),
    )


def cos_sin(turns):
    f = turns - jnp.round(turns)
    g = f * f
    s, c = SIN[-1], COS[-1]
    for low in SIN[-2::-1]:
        s = s * g + low
    for low in COS[-2::-1]:
        c = c * g + low
    s = s * f
    twice = s + s
    return 1.0 - twice * s, twice * c


def core_of():
    return lax.axis_index("dom") % 2


def count_kernel(part, neighbours_ref, count_ref, number_ref, named):
    slot = lax.broadcasted_iota(jnp.int32, neighbours_ref.shape, 0)
    named[...] = jnp.where(slot < count_ref[...], neighbours_ref[...], -1)
    rows, atoms = number_ref.shape
    ghosts = rows // 2
    core = core_of()

    def chunk(c, carry):
        start = pl.multiple_of(c * ROWS, ROWS)
        row = start + part * rows
        swap = jnp.where(core == 0, ghosts, 0)
        shift = jnp.where(row >= atoms + ghosts, -swap, jnp.where(row >= atoms, swap, 0))
        local = lax.broadcasted_iota(jnp.int32, (ROWS, atoms), 0) + (row + shift)
        total = jnp.zeros((ROWS, atoms), F32)
        for k in range(NEIGH):
            total = total + jnp.where(local == named[k : k + 1, :], 1.0, 0.0)
        number_ref[pl.ds(start, ROWS), :] = total
        return carry

    lax.fori_loop(0, rows // ROWS, chunk, 0)


def near_far_lists(lists_ref):
    core = core_of()
    return [lists_ref[pl.ds(1 - core, 1), :], lists_ref[pl.ds(core, 1), :]]


def gather_rows(columns, list_row, count):
    atoms, listed = columns.shape[0], list_row.shape[1]
    hit = lax.broadcasted_iota(jnp.int32, (atoms, listed), 0) == list_row
    return [
        jnp.sum(jnp.where(hit, columns[:, a : a + 1], 0.0), axis=0, keepdims=True)
        for a in range(count)
    ]


def send_rows(position_rows, species_row, lists, near_ref, far_ref, wide):
    wide[...] = jnp.zeros_like(wide)
    for a in range(3):
        wide[a : a + 1, :] = position_rows[a]
    wide[3:4, :] = species_row
    columns = wide[...].T
    for out, listed in zip((near_ref, far_ref), lists):
        for a, row in enumerate(gather_rows(columns, listed, 4)):
            out[a : a + 1, :] = row


def first_kernel(position_ref, species_ref, lists_ref, near_ref, far_ref, wide):
    rows = [position_ref[a] for a in range(3)]
    lists = near_far_lists(lists_ref)
    send_rows(rows, species_ref[...].astype(F32), lists, near_ref, far_ref, wide)


def update_kernel(
    last,
    force_ref,
    near_back_ref,
    far_back_ref,
    lists_ref,
    position_ref,
    velocity_ref,
    below_ref,
    above_ref,
    species_ref,
    new_position_ref,
    new_velocity_ref,
    *rest,
):
    atoms = position_ref.shape[2]
    listed = lists_ref.shape[1]
    wide = rest[-1]
    back = rest[-2]
    lists = near_far_lists(lists_ref)
    extra = [0.0, 0.0, 0.0]
    for names, ref in zip(lists, (near_back_ref, far_back_ref)):
        back[...] = jnp.zeros_like(back)
        back[0:3, :] = ref[...]
        back[3:4, :] = names.astype(F32)
        values = back[...].T
        hit = lax.broadcasted_iota(jnp.int32, (listed, atoms), 1).astype(F32) == values[:, 3:4]
        for a in range(3):
            extra[a] = extra[a] + jnp.sum(
                jnp.where(hit, values[:, a : a + 1], 0.0), axis=0, keepdims=True
            )
    species = species_ref[...]
    mass = jnp.where(species == 0, 16.0, 1.0)
    rows = []
    for a in range(3):
        here = position_ref[a]
        chain = 2.0 * here - below_ref[a] - above_ref[a]
        total = force_ref[a : a + 1, :] + extra[a] - KAPPA * mass * chain
        velocity = velocity_ref[a] + DT * (total / mass)
        place = here + DT * velocity
        new_velocity_ref[a] = velocity
        new_position_ref[a] = place
        rows.append(place)
    if not last:
        send_rows(rows, species.astype(F32), lists, rest[0], rest[1], wide)


def each(count, body, unroll=4, carry=0):
    return lax.fori_loop(0, count // ROWS, body, carry, unroll=min(unroll, count // ROWS))


def chunk_rows(c, first=0):
    return pl.ds(pl.multiple_of(first + c * ROWS, ROWS), ROWS)


def own_kernel(
    position_ref,
    species_ref,
    projection_ref,
    shift_ref,
    cols,
    waves,
    turned,
    rows_in,
):
    own = position_ref.shape[2]
    features = projection_ref.shape[2]
    rows_in[...] = jnp.zeros_like(rows_in)
    for a in range(3):
        rows_in[a : a + 1, :] = position_ref[a]
    rows_in[3:4, :] = species_ref[...].astype(F32)
    cols[...] = rows_in[...].T

    shift_cos, shift_sin = cos_sin(shift_ref[...] * TURN)
    for block in range(features // FB):
        mine = slice(block * FB, (block + 1) * FB)
        base = block * 4 * FB
        wave = [
            [projection_ref[a, s : s + 1, mine] * TURN for a in range(3)] for s in range(2)
        ]
        turn_cos = [shift_cos[s : s + 1, mine] for s in range(2)]
        turn_sin = [shift_sin[s : s + 1, mine] for s in range(2)]

        def own_waves(c, carry):
            rows = chunk_rows(c)
            there = cols[rows, :]
            x, y, z = (jnp.broadcast_to(there[:, a : a + 1], (ROWS, FB)) for a in range(3))
            second = jnp.broadcast_to(there[:, 3:4], (ROWS, FB)) > 0.5
            for s in range(2):
                cos, sin = cos_sin(x * wave[s][0] + y * wave[s][1] + z * wave[s][2])
                at = base + s * 2 * FB
                turned[rows, at : at + FB] = turn_cos[s] * cos + turn_sin[s] * sin
                turned[rows, at + FB : at + 2 * FB] = turn_sin[s] * cos - turn_cos[s] * sin
                if s == 0:
                    cos, sin = jnp.where(second, 0.0, cos), jnp.where(second, 0.0, sin)
                else:
                    cos, sin = jnp.where(second, cos, 0.0), jnp.where(second, sin, 0.0)
                waves[rows, at : at + FB] = cos.astype(BF16)
                waves[rows, at + FB : at + 2 * FB] = sin.astype(BF16)
            return carry

        each(own, own_waves)


def weigh_kernel(
    position_ref,
    near_ref,
    far_ref,
    own_cols,
    projection_ref,
    *rest,
):
    *numbers, ghost_cols, weight, weight_turned, waves, rows_in = rest
    own = position_ref.shape[2]
    sent = near_ref.shape[1]
    features = projection_ref.shape[2]

    rows_in[...] = jnp.zeros_like(rows_in)
    rows_in[0:4, 0:sent] = near_ref[...]
    rows_in[0:4, sent : 2 * sent] = far_ref[...]
    ghost_cols[...] = rows_in[...].T
    here = [position_ref[a] for a in range(3)]

    for k, number_ref in enumerate(numbers):
        first = k * number_ref.shape[0]
        cols, skip = (own_cols, first) if first < own else (ghost_cols, first - own)

        def weigh(c, carry):
            there = cols[chunk_rows(c, skip), :]
            square = 0.0
            for a in range(3):
                d = there[:, a : a + 1] - here[a]
                square = square + d * d
            weight[chunk_rows(c, first), :] = number_ref[chunk_rows(c), :] * jnp.exp(
                square * (-1.0 / (2.0 * WIDTH * WIDTH))
            )
            return carry

        each(number_ref.shape[0], weigh)
    weight_turned[...] = weight[...].T.astype(BF16)

    for block in range(features // FB):
        mine = slice(block * FB, (block + 1) * FB)
        base = block * 4 * FB
        wave = [
            [projection_ref[a, s : s + 1, mine] * TURN for a in range(3)] for s in range(2)
        ]

        def ghost_waves(c, carry):
            rows = chunk_rows(c)
            there = ghost_cols[rows, :]
            x, y, z = (jnp.broadcast_to(there[:, a : a + 1], (ROWS, FB)) for a in range(3))
            second = jnp.broadcast_to(there[:, 3:4], (ROWS, FB)) > 0.5
            px, py, pz = (jnp.where(second, wave[1][a], wave[0][a]) for a in range(3))
            cos, sin = cos_sin(x * px + y * py + z * pz)
            for s in range(2):
                at = base + s * 2 * FB
                for k, part in enumerate((cos, sin)):
                    if s == 0:
                        part = jnp.where(second, 0.0, part)
                    else:
                        part = jnp.where(second, part, 0.0)
                    waves[rows, at + k * FB : at + (k + 1) * FB] = part.astype(BF16)
            return carry

        each(2 * sent, ghost_waves)


def describe_kernel(
    weight_turned,
    own_waves,
    ghost_waves,
    turned,
    sines,
    low,
    sums,
):
    own = weight_turned.shape[0]
    features = low.shape[1]
    for block in range(features // FB):
        mine = slice(block * FB, (block + 1) * FB)
        base = block * 4 * FB
        sums[...] = jnp.dot(
            weight_turned[:, 0:own], own_waves[:, base : base + 4 * FB], preferred_element_type=F32
        ) + jnp.dot(
            weight_turned[:, own:], ghost_waves[:, base : base + 4 * FB], preferred_element_type=F32
        )

        def describe(c, carry):
            rows = chunk_rows(c)
            total = 0.0
            for s in range(2):
                at = base + s * 2 * FB
                tr, ti = turned[rows, at : at + FB], turned[rows, at + FB : at + 2 * FB]
                ur = sums[rows, s * 2 * FB : s * 2 * FB + FB]
                ui = sums[rows, s * 2 * FB + FB : s * 2 * FB + 2 * FB]
                total = total + (tr * ur - ti * ui)
                first = s * features + block * FB
                sines[rows, first : first + FB] = tr * ui + ti * ur
            low[rows, mine] = total.astype(BF16)
            return carry

        each(own, describe)


def fold(value):
    total = value[:, 0:LANES]
    for k in range(1, value.shape[1] // LANES):
        total = total + value[:, k * LANES : (k + 1) * LANES]
    return total


def pull_rows(first, cols, waves, weight, spread, projection_ref, here, parts, back, product):
    count = cols.shape[0]
    features = projection_ref.shape[2]
    held = weight[first : first + count, :].astype(BF16)
    for block in range(features // FB):
        mine = slice(block * FB, (block + 1) * FB)
        base = block * 4 * FB
        raw = [[projection_ref[a, s : s + 1, mine] for a in range(3)] for s in range(2)]
        back[...] = jnp.dot(held, spread[:, base : base + 4 * FB], preferred_element_type=F32)

        def pull(c, carry):
            rows = chunk_rows(c)
            second = jnp.broadcast_to(cols[rows, 3:4], (ROWS, FB)) > 0.5
            total = 0.0
            for s in range(2):
                at = base + s * 2 * FB
                er = waves[rows, at : at + FB].astype(F32)
                ei = waves[rows, at + FB : at + 2 * FB].astype(F32)
                vr = back[rows, s * 2 * FB : s * 2 * FB + FB]
                vi = back[rows, s * 2 * FB + FB : s * 2 * FB + 2 * FB]
                total = total + (ei * vr - er * vi)
            for a in range(3):
                coeff = jnp.where(second, raw[1][a], raw[0][a])
                parts[a, rows, :] = parts[a, rows, :] + fold(total * coeff)
            return carry

        each(count, pull)

    product[...] = lax.dot_general(
        waves[...], spread[...], (((1,), (1,)), ((), ())), preferred_element_type=F32
    )

    def along(c, carry):
        rows = chunk_rows(c)
        there = cols[rows, :]
        z = weight[chunk_rows(c, first), :] * product[rows, :] * (1.0 / (WIDTH * WIDTH))
        out = []
        for a in range(3):
            pull_a = z * (there[:, a : a + 1] - here[a])
            parts[a, rows, :] = parts[a, rows, :] + fold(pull_a)
            total = pull_a[0:8]
            for k in range(1, ROWS // 8):
                total = total + pull_a[8 * k : 8 * k + 8]
            out.append(carry[a] + total)
        return tuple(out)

    start = tuple(jnp.zeros((8, here[0].shape[1]), F32) for _ in range(3))
    return each(count, along, carry=start)


def ghost_force_kernel(
    low,
    half_ref,
    other_ref,
    own_cols,
    turned,
    weight,
    waves,
    cols,
    position_ref,
    projection_ref,
    grad,
    spread,
    centre_ref,
    near_ref,
    far_ref,
    back,
    product,
    parts,
):
    own, features = grad.shape
    sent = near_ref.shape[1]
    here = [position_ref[a] for a in range(3)]
    mine_is = core_of().astype(F32)
    grad[...] = jnp.where(
        own_cols[:, 3:4] == mine_is,
        jnp.dot(low[...], half_ref[...], preferred_element_type=F32),
        jnp.dot(low[...], other_ref[...], preferred_element_type=F32),
    )
    for block in range(features // FB):
        mine = slice(block * FB, (block + 1) * FB)
        base = block * 4 * FB

        def spread_out(c, carry):
            rows = chunk_rows(c)
            g = grad[rows, mine]
            for s in range(2):
                at = base + s * 2 * FB
                spread[rows, at : at + FB] = (g * turned[rows, at : at + FB]).astype(BF16)
                spread[rows, at + FB : at + 2 * FB] = (
                    -g * turned[rows, at + FB : at + 2 * FB]
                ).astype(BF16)
            return carry

        each(own, spread_out)

    parts[...] = jnp.zeros_like(parts)
    centre = pull_rows(
        own, cols, waves, weight, spread, projection_ref, here, parts, back, product
    )
    for a in range(3):
        row = jnp.sum(parts[a].T, axis=0, keepdims=True)
        centre_ref[a : a + 1, :] = jnp.sum(centre[a], axis=0, keepdims=True)
        near_ref[a : a + 1, :] = row[:, 0:sent]
        far_ref[a : a + 1, :] = row[:, sent:]


def own_force_kernel(
    grad,
    spread,
    sines,
    waves,
    weight,
    cols,
    position_ref,
    centre_ref,
    projection_ref,
    force_ref,
    back,
    product,
    parts,
):
    own, features = grad.shape
    here = [position_ref[a] for a in range(3)]
    raw = [[projection_ref[a, s : s + 1, :] for a in range(3)] for s in range(2)]

    def turn(c, carry):
        rows = chunk_rows(c)
        g = grad[rows, :]
        t0 = g * sines[rows, 0:features]
        t1 = g * sines[rows, features : 2 * features]
        for a in range(3):
            parts[a, rows, :] = -fold(t0 * raw[0][a] + t1 * raw[1][a])
        return carry

    each(own, turn, 2)
    centre = pull_rows(
        0, cols, waves, weight, spread, projection_ref, here, parts, back, product
    )
    for a in range(3):
        row = jnp.sum(parts[a].T, axis=0, keepdims=True)
        force_ref[a : a + 1, :] = (
            row - jnp.sum(centre[a], axis=0, keepdims=True) - centre_ref[a : a + 1, :]
        )


def passed_along(block, axis, distance):
    devices = range(lax.axis_size(axis))
    route = [((i - distance) % len(devices), i) for i in devices]
    return lax.ppermute(block, axis, route)


def routed(block, axis, source):
    return lax.ppermute(block, axis, [(source(i), i) for i in range(lax.axis_size(axis))])


def near_pair(block):
    return routed(block, "dom", lambda i: i ^ 1)


def far_pair(block):
    return routed(block, "dom", lambda i: (i - 1 + i % 2 * 2) % lax.axis_size("dom"))


def after(value, *others):
    return lax.optimization_barrier((value, others))[0]


def matrix_part(points, point_weights):
    dom = lax.axis_index("dom")
    which, height = dom % 2, points.shape[2] // 8
    p = lax.dynamic_index_in_dim(points, which, 0, keepdims=False).astype(F32)
    w = lax.dynamic_index_in_dim(point_weights, which, 0, keepdims=False).astype(F32)
    left = lax.dynamic_slice_in_dim(p, (dom // 4 * 2 + dom // 2 % 2) * height, height, axis=1)
    return lax.dot_general(
        left * (2.0 * w)[:, None],
        p,
        (((0,), (0,)), ((), ())),
        precision=lax.Precision.HIGHEST,
        preferred_element_type=F32,
    )


def add_kernel(part_ref, other_ref, *outs):
    total = part_ref[...] + other_ref[...].astype(F32)
    for out in outs:
        out[...] = total.astype(out.dtype)


def pair_kernel(held_ref, other_ref, out_ref):
    rows = held_ref.shape[0]
    bit = lax.axis_index("dom") // 2 % 2
    out_ref[pl.ds(pl.multiple_of(bit * rows, rows), rows), :] = held_ref[...]
    out_ref[pl.ds(pl.multiple_of((1 - bit) * rows, rows), rows), :] = other_ref[...]


def ring_kernel(*refs):
    *pieces, out_ref = refs
    rows = pieces[0].shape[0]
    height = lax.axis_index("dom") // 4
    for k, piece in enumerate(pieces):
        place = (height + 4 - k) % 4
        out_ref[pl.ds(pl.multiple_of(place * rows, rows), rows), :] = piece[...]


def shards(
    positions,
    velocities,
    species,
    neighbours,
    neighbour_count,
    send_lists,
    projection,
    phase_shift,
    points,
    point_weights,
):
    own, sent = positions.shape[2], send_lists.shape[1]
    ghosts = 2 * sent
    everyone = own + ghosts
    features = points.shape[2]
    shape = jax.ShapeDtypeStruct
    species = species.reshape(1, own)
    position, velocity = positions.transpose(1, 0, 2), velocities.transpose(1, 0, 2)
    projection = projection.transpose(1, 0, 2)
    sends = (shape((4, sent), F32),) * 2
    wide = pltpu.VMEM((LANES, own), F32)
    slab = (features // 8, features)
    counts = neighbour_count.reshape(1, own)

    def count(part, neighbours):
        return call(
            functools.partial(count_kernel, part),
            shape((ghosts, own), F32),
            [pltpu.VMEM((NEIGH, own), jnp.int32)],
        )(neighbours, counts)

    own_call = call(
        own_kernel,
        (
            shape((own, LANES), F32),
            shape((own, 4 * features), BF16),
            shape((own, 4 * features), F32),
        ),
        [wide],
        LIMIT,
    )
    weigh_call = call(
        weigh_kernel,
        (
            shape((ghosts, LANES), F32),
            shape((everyone, own), F32),
            shape((own, everyone), BF16),
            shape((ghosts, 4 * features), BF16),
        ),
        [pltpu.VMEM((LANES, ghosts), F32)],
        LIMIT,
    )
    describe_call = call(
        describe_kernel,
        (shape((own, 2 * features), F32), shape((own, features), BF16)),
        [pltpu.VMEM((own, 4 * FB), F32)],
        LIMIT,
    )
    ghost_force_call = call(
        ghost_force_kernel,
        (
            shape((own, features), F32),
            shape((own, 4 * features), BF16),
            shape((3, own), F32),
            shape((3, sent), F32),
            shape((3, sent), F32),
        ),
        [
            pltpu.VMEM((ghosts, 4 * FB), F32),
            pltpu.VMEM((ghosts, own), F32),
            pltpu.VMEM((3, ghosts, LANES), F32),
        ],
        LIMIT,
    )
    own_force_call = call(
        own_force_kernel,
        shape((3, own), F32),
        [
            pltpu.VMEM((own, 4 * FB), F32),
            pltpu.VMEM((own, own), F32),
            pltpu.VMEM((3, own, LANES), F32),
        ],
        LIMIT,
    )

    above = passed_along(position, "bead", -1)
    to_near, to_far = call(first_kernel, sends, [wide])(position, species, send_lists)
    part = after(matrix_part(points, point_weights), to_near, to_far)
    for step in range(STEPS):
        last = step == STEPS - 1
        if step == 0:
            other = routed(part, "bead", lambda i: i ^ 4)
            to_far = after(to_far, part)
        from_far = far_pair(to_far)
        from_near = near_pair(to_near)
        cols, waves, turned = own_call(position, species, projection, phase_shift)
        if step == 0:
            number = []
            part, held = call(add_kernel, (shape(slab, F32), shape(slab, BF16)))(
                part, after(other, cols, from_far, from_near)
            )
            other = routed(held, "bead", lambda i: i ^ 1)
            number.append(count(0, after(neighbours, held)))
            part, held = call(add_kernel, (shape(slab, F32), shape(slab, BF16)))(
                part, after(other, number[-1])
            )
            other = routed(held, "bead", lambda i: i ^ 2)
            number.append(count(1, after(neighbours, held)))
            held = call(add_kernel, (shape(slab, BF16),))(part, after(other, number[-1]))[0]
            other = routed(held, "dom", lambda i: i ^ 2)
            number.append(count(2, after(neighbours, held)))
            state = weigh_call(position, from_near, from_far, cols, projection, *number)
            ghost_cols, weight, weight_turned, ghost_waves = state
            held = call(pair_kernel, shape((2 * slab[0], features), BF16))(
                held, after(other, *state)
            )
            pieces = [held] + [routed(held, "dom", lambda i: (i - 4 * k) % 16) for k in (1, 2, 3)]
            sines, low = describe_call(after(weight_turned, held), waves, ghost_waves, turned)
            half = call(ring_kernel, shape((features, features), BF16))(
                pieces[0], *[after(piece, low) for piece in pieces[1:]]
            )
            other_half = near_pair(half)
            below = passed_along(after(position, other_half), "bead", 1)
        else:
            above = passed_along(after(position, cols, from_far, from_near), "bead", -1)
            ghost_cols, weight, weight_turned, ghost_waves = weigh_call(
                position, from_near, from_far, cols, projection, *number
            )
            sines, low = describe_call(weight_turned, waves, ghost_waves, turned)
            below = passed_along(after(position, low), "bead", 1)
        grad, spread, centre, near_force, far_force = ghost_force_call(
            low,
            half,
            other_half,
            cols,
            turned,
            weight,
            ghost_waves,
            ghost_cols,
            position,
            projection,
        )
        far_back = far_pair(far_force)
        near_back = near_pair(near_force)
        force = own_force_call(
            grad, spread, sines, waves, weight, cols, position, centre, projection
        )
        moved = shape(position.shape, F32)
        position, velocity, *rest = call(
            functools.partial(update_kernel, last),
            (moved, moved) + (() if last else sends),
            [pltpu.VMEM((LANES, sent), F32), wide],
        )(
            force,
            near_back,
            far_back,
            send_lists,
            position,
            velocity,
            below,
            above,
            species,
        )
        if not last:
            to_near, to_far = rest
    return (position.transpose(1, 0, 2), velocity.transpose(1, 0, 2))


def solution(mesh):
    placed = (
        P("bead", None, "dom"),
        P("bead", None, "dom"),
        P("dom"),
        P(None, "dom"),
        P("dom"),
        P(None, "dom"),
        P(),
        P(),
        P(None, "bead", None),
        P(None, "bead"),
    )
    return jax.shard_map(
        shards,
        mesh=mesh,
        in_specs=placed,
        out_specs=(P("bead", None, "dom"), P("bead", None, "dom")),
        check_vma=False,
    )
```

```python
import functools

import jax
import jax.numpy as jnp
from jax import lax
from jax.experimental import pallas as pl
from jax.experimental.pallas import tpu as pltpu
from jax.sharding import PartitionSpec as P

NEIGH = 32
STEPS = 2

WIDTH = 1.5
DT = 0.1
KAPPA = 0.5

F32, BF16 = jnp.float32, jnp.bfloat16
LANES = 128
ROWS = 32
FB = 256
TURN = 0.15915494309189535
SIN = (3.1415927410125732, -5.167710304260254, 2.550077438354492, -0.5982903838157654, 0.07765591144561768)
COS = (0.9999999403953552, -4.934792995452881, 4.05841064453125, -1.3318729400634766, 0.21968242526054382)
VMEM = pl.BlockSpec(memory_space=pltpu.VMEM)
MIB = 1024 * 1024
LIMIT = 16


def call(body, outs, scratch=(), limit=8):
    return pl.pallas_call(
        body,
        out_shape=outs,
        out_specs=jax.tree.map(lambda _: VMEM, outs),
        scratch_shapes=scratch,
        compiler_params=pltpu.CompilerParams(vmem_limit_bytes=limit * MIB),
    )


def cos_sin(turns):
    f = turns - jnp.round(turns)
    g = f * f
    s, c = SIN[-1], COS[-1]
    for low in SIN[-2::-1]:
        s = s * g + low
    for low in COS[-2::-1]:
        c = c * g + low
    s = s * f
    twice = s + s
    return 1.0 - twice * s, twice * c


def core_of():
    return lax.axis_index("dom") % 2


def count_kernel(part, neighbours_ref, count_ref, number_ref, named):
    rows, atoms = number_ref.shape
    slot = lax.broadcasted_iota(jnp.int32, neighbours_ref.shape, 0)
    row = jnp.where(slot < count_ref[...], neighbours_ref[...] - part * rows, -1)
    if part * rows >= atoms:
        swapped = jnp.where(row >= rows // 2, row - rows // 2, row + rows // 2)
        row = jnp.where((core_of() == 0) & (row >= 0), swapped, row)
    named[...] = jnp.where((row >= 0) & (row < rows), row, -1).astype(F32)
    one, zero = jnp.ones((), BF16), jnp.zeros((), BF16)
    step = 2 * ROWS
    for start in range(0, rows, step):
        local = (lax.broadcasted_iota(jnp.int32, (step, atoms), 0) + start).astype(F32).astype(BF16)
        total = jnp.zeros((step, atoms), BF16)
        for k in range(NEIGH):
            total = total + jnp.where(local == named[k : k + 1, :].astype(BF16), one, zero)
        number_ref[start : start + step, :] = total.astype(F32)


def near_far_lists(lists_ref):
    core = core_of()
    return [lists_ref[pl.ds(1 - core, 1), :], lists_ref[pl.ds(core, 1), :]]


def gather_rows(columns, list_row, count):
    atoms, listed = columns.shape[0], list_row.shape[1]
    hit = lax.broadcasted_iota(jnp.int32, (atoms, listed), 0) == list_row
    return [
        jnp.sum(jnp.where(hit, columns[:, a : a + 1], 0.0), axis=0, keepdims=True)
        for a in range(count)
    ]


def send_rows(position_rows, species_row, lists, near_ref, far_ref, wide):
    wide[...] = jnp.zeros_like(wide)
    for a in range(3):
        wide[a : a + 1, :] = position_rows[a]
    wide[3:4, :] = species_row
    columns = wide[...].T
    for out, listed in zip((near_ref, far_ref), lists):
        for a, row in enumerate(gather_rows(columns, listed, 4)):
            out[a : a + 1, :] = row


def first_kernel(position_ref, species_ref, lists_ref, near_ref, far_ref, wide):
    rows = [position_ref[a] for a in range(3)]
    lists = near_far_lists(lists_ref)
    send_rows(rows, species_ref[...].astype(F32), lists, near_ref, far_ref, wide)


def update_kernel(
    last,
    force_ref,
    near_back_ref,
    far_back_ref,
    lists_ref,
    position_ref,
    velocity_ref,
    below_ref,
    above_ref,
    species_ref,
    new_position_ref,
    new_velocity_ref,
    *rest,
):
    atoms = position_ref.shape[2]
    listed = lists_ref.shape[1]
    wide = rest[-1]
    back = rest[-2]
    lists = near_far_lists(lists_ref)
    extra = [0.0, 0.0, 0.0]
    for names, ref in zip(lists, (near_back_ref, far_back_ref)):
        back[...] = jnp.zeros_like(back)
        back[0:3, :] = ref[...]
        back[3:4, :] = names.astype(F32)
        values = back[...].T
        hit = lax.broadcasted_iota(jnp.int32, (listed, atoms), 1).astype(F32) == values[:, 3:4]
        for a in range(3):
            extra[a] = extra[a] + jnp.sum(
                jnp.where(hit, values[:, a : a + 1], 0.0), axis=0, keepdims=True
            )
    species = species_ref[...]
    mass = jnp.where(species == 0, 16.0, 1.0)
    rows = []
    for a in range(3):
        here = position_ref[a]
        chain = 2.0 * here - below_ref[a] - above_ref[a]
        total = force_ref[a : a + 1, :] + extra[a] - KAPPA * mass * chain
        velocity = velocity_ref[a] + DT * (total / mass)
        place = here + DT * velocity
        new_velocity_ref[a] = velocity
        new_position_ref[a] = place
        rows.append(place)
    if not last:
        send_rows(rows, species.astype(F32), lists, rest[0], rest[1], wide)


def each(count, body, carry=0):
    for c in range(count // ROWS):
        carry = body(c, carry)
    return carry


def chunk_rows(c, first=0):
    return slice(first + c * ROWS, first + (c + 1) * ROWS)


def own_kernel(
    position_ref,
    species_ref,
    projection_ref,
    shift_ref,
    cols,
    waves,
    turned,
    rows_in,
):
    own = position_ref.shape[2]
    features = projection_ref.shape[2]
    rows_in[...] = jnp.zeros_like(rows_in)
    for a in range(3):
        rows_in[a : a + 1, :] = position_ref[a]
    rows_in[3:4, :] = species_ref[...].astype(F32)
    cols[...] = rows_in[...].T

    shift_cos, shift_sin = cos_sin(shift_ref[...] * TURN)
    for block in range(features // FB):
        mine = slice(block * FB, (block + 1) * FB)
        base = block * 4 * FB
        wave = [
            [projection_ref[a, s : s + 1, mine] * TURN for a in range(3)] for s in range(2)
        ]
        turn_cos = [shift_cos[s : s + 1, mine] for s in range(2)]
        turn_sin = [shift_sin[s : s + 1, mine] for s in range(2)]

        def own_waves(c, carry):
            rows = chunk_rows(c)
            there = cols[rows, :]
            x, y, z = (jnp.broadcast_to(there[:, a : a + 1], (ROWS, FB)) for a in range(3))
            second = jnp.broadcast_to(there[:, 3:4], (ROWS, FB)) > 0.5
            for s in range(2):
                cos, sin = cos_sin(x * wave[s][0] + y * wave[s][1] + z * wave[s][2])
                at = base + s * 2 * FB
                turned[rows, at : at + FB] = turn_cos[s] * cos + turn_sin[s] * sin
                turned[rows, at + FB : at + 2 * FB] = turn_sin[s] * cos - turn_cos[s] * sin
                if s == 0:
                    cos, sin = jnp.where(second, 0.0, cos), jnp.where(second, 0.0, sin)
                else:
                    cos, sin = jnp.where(second, cos, 0.0), jnp.where(second, sin, 0.0)
                waves[rows, at : at + FB] = cos.astype(BF16)
                waves[rows, at + FB : at + 2 * FB] = sin.astype(BF16)
            return carry

        each(own, own_waves)


def weigh_kernel(
    position_ref,
    near_ref,
    far_ref,
    own_cols,
    projection_ref,
    *rest,
):
    *numbers, ghost_cols, weight, weight_turned, waves, rows_in = rest
    own = position_ref.shape[2]
    sent = near_ref.shape[1]
    features = projection_ref.shape[2]

    rows_in[...] = jnp.zeros_like(rows_in)
    rows_in[0:4, 0:sent] = near_ref[...]
    rows_in[0:4, sent : 2 * sent] = far_ref[...]
    ghost_cols[...] = rows_in[...].T
    here = [position_ref[a] for a in range(3)]

    for k, number_ref in enumerate(numbers):
        first = k * number_ref.shape[0]
        cols, skip = (own_cols, first) if first < own else (ghost_cols, first - own)

        def weigh(c, carry):
            there = cols[chunk_rows(c, skip), :]
            square = 0.0
            for a in range(3):
                d = there[:, a : a + 1] - here[a]
                square = square + d * d
            weight[chunk_rows(c, first), :] = number_ref[chunk_rows(c), :] * jnp.exp(
                square * (-1.0 / (2.0 * WIDTH * WIDTH))
            )
            return carry

        each(number_ref.shape[0], weigh)
    weight_turned[...] = weight[...].T.astype(BF16)

    for block in range(features // FB):
        mine = slice(block * FB, (block + 1) * FB)
        base = block * 4 * FB
        wave = [
            [projection_ref[a, s : s + 1, mine] * TURN for a in range(3)] for s in range(2)
        ]

        def ghost_waves(c, carry):
            rows = chunk_rows(c)
            there = ghost_cols[rows, :]
            x, y, z = (jnp.broadcast_to(there[:, a : a + 1], (ROWS, FB)) for a in range(3))
            second = jnp.broadcast_to(there[:, 3:4], (ROWS, FB)) > 0.5
            px, py, pz = (jnp.where(second, wave[1][a], wave[0][a]) for a in range(3))
            cos, sin = cos_sin(x * px + y * py + z * pz)
            for s in range(2):
                at = base + s * 2 * FB
                for k, part in enumerate((cos, sin)):
                    if s == 0:
                        part = jnp.where(second, 0.0, part)
                    else:
                        part = jnp.where(second, part, 0.0)
                    waves[rows, at + k * FB : at + (k + 1) * FB] = part.astype(BF16)
            return carry

        each(2 * sent, ghost_waves)


def describe_kernel(
    weight_turned,
    own_waves,
    ghost_waves,
    turned,
    sines,
    low,
    sums,
):
    own = weight_turned.shape[0]
    features = low.shape[1]
    for block in range(features // FB):
        mine = slice(block * FB, (block + 1) * FB)
        base = block * 4 * FB
        sums[...] = jnp.dot(
            weight_turned[:, 0:own], own_waves[:, base : base + 4 * FB], preferred_element_type=F32
        ) + jnp.dot(
            weight_turned[:, own:], ghost_waves[:, base : base + 4 * FB], preferred_element_type=F32
        )

        def describe(c, carry):
            rows = chunk_rows(c)
            total = 0.0
            for s in range(2):
                at = base + s * 2 * FB
                tr, ti = turned[rows, at : at + FB], turned[rows, at + FB : at + 2 * FB]
                ur = sums[rows, s * 2 * FB : s * 2 * FB + FB]
                ui = sums[rows, s * 2 * FB + FB : s * 2 * FB + 2 * FB]
                total = total + (tr * ur - ti * ui)
                first = s * features + block * FB
                sines[rows, first : first + FB] = tr * ui + ti * ur
            low[rows, mine] = total.astype(BF16)
            return carry

        each(own, describe)


def fold(value):
    total = value[:, 0:LANES]
    for k in range(1, value.shape[1] // LANES):
        total = total + value[:, k * LANES : (k + 1) * LANES]
    return total


def pull_rows(first, cols, waves, weight, spread, projection_ref, here, parts, back, product):
    count = cols.shape[0]
    features = projection_ref.shape[2]
    held = weight[first : first + count, :].astype(BF16)
    for block in range(features // FB):
        mine = slice(block * FB, (block + 1) * FB)
        base = block * 4 * FB
        raw = [[projection_ref[a, s : s + 1, mine] for a in range(3)] for s in range(2)]
        back[...] = jnp.dot(held, spread[:, base : base + 4 * FB], preferred_element_type=F32)

        def pull(c, carry):
            rows = chunk_rows(c)
            second = jnp.broadcast_to(cols[rows, 3:4], (ROWS, FB)) > 0.5
            total = 0.0
            for s in range(2):
                at = base + s * 2 * FB
                er = waves[rows, at : at + FB].astype(F32)
                ei = waves[rows, at + FB : at + 2 * FB].astype(F32)
                vr = back[rows, s * 2 * FB : s * 2 * FB + FB]
                vi = back[rows, s * 2 * FB + FB : s * 2 * FB + 2 * FB]
                total = total + (ei * vr - er * vi)
            for a in range(3):
                coeff = jnp.where(second, raw[1][a], raw[0][a])
                parts[a, rows, :] = parts[a, rows, :] + fold(total * coeff)
            return carry

        each(count, pull)

    product[...] = lax.dot_general(
        waves[...], spread[...], (((1,), (1,)), ((), ())), preferred_element_type=F32
    )

    def along(c, carry):
        rows = chunk_rows(c)
        there = cols[rows, :]
        z = weight[chunk_rows(c, first), :] * product[rows, :] * (1.0 / (WIDTH * WIDTH))
        out = []
        for a in range(3):
            pull_a = z * (there[:, a : a + 1] - here[a])
            parts[a, rows, :] = parts[a, rows, :] + fold(pull_a)
            total = pull_a[0:8]
            for k in range(1, ROWS // 8):
                total = total + pull_a[8 * k : 8 * k + 8]
            out.append(carry[a] + total)
        return tuple(out)

    start = tuple(jnp.zeros((8, here[0].shape[1]), F32) for _ in range(3))
    return each(count, along, carry=start)


def ghost_force_kernel(
    low,
    half_ref,
    other_ref,
    own_cols,
    turned,
    weight,
    waves,
    cols,
    position_ref,
    projection_ref,
    grad,
    spread,
    centre_ref,
    near_ref,
    far_ref,
    back,
    product,
    parts,
):
    own, features = grad.shape
    sent = near_ref.shape[1]
    here = [position_ref[a] for a in range(3)]
    mine_is = core_of().astype(F32)
    grad[...] = jnp.where(
        own_cols[:, 3:4] == mine_is,
        jnp.dot(low[...], half_ref[...], preferred_element_type=F32),
        jnp.dot(low[...], other_ref[...], preferred_element_type=F32),
    )
    for block in range(features // FB):
        mine = slice(block * FB, (block + 1) * FB)
        base = block * 4 * FB

        def spread_out(c, carry):
            rows = chunk_rows(c)
            g = grad[rows, mine]
            for s in range(2):
                at = base + s * 2 * FB
                spread[rows, at : at + FB] = (g * turned[rows, at : at + FB]).astype(BF16)
                spread[rows, at + FB : at + 2 * FB] = (
                    -g * turned[rows, at + FB : at + 2 * FB]
                ).astype(BF16)
            return carry

        each(own, spread_out)

    parts[...] = jnp.zeros_like(parts)
    centre = pull_rows(
        own, cols, waves, weight, spread, projection_ref, here, parts, back, product
    )
    for a in range(3):
        row = jnp.sum(parts[a].T, axis=0, keepdims=True)
        centre_ref[a : a + 1, :] = jnp.sum(centre[a], axis=0, keepdims=True)
        near_ref[a : a + 1, :] = row[:, 0:sent]
        far_ref[a : a + 1, :] = row[:, sent:]


def own_force_kernel(
    grad,
    spread,
    sines,
    waves,
    weight,
    cols,
    position_ref,
    centre_ref,
    projection_ref,
    force_ref,
    back,
    product,
    parts,
):
    own, features = grad.shape
    here = [position_ref[a] for a in range(3)]
    raw = [[projection_ref[a, s : s + 1, :] for a in range(3)] for s in range(2)]

    def turn(c, carry):
        rows = chunk_rows(c)
        g = grad[rows, :]
        t0 = g * sines[rows, 0:features]
        t1 = g * sines[rows, features : 2 * features]
        for a in range(3):
            parts[a, rows, :] = -fold(t0 * raw[0][a] + t1 * raw[1][a])
        return carry

    each(own, turn)
    centre = pull_rows(
        0, cols, waves, weight, spread, projection_ref, here, parts, back, product
    )
    for a in range(3):
        row = jnp.sum(parts[a].T, axis=0, keepdims=True)
        force_ref[a : a + 1, :] = (
            row - jnp.sum(centre[a], axis=0, keepdims=True) - centre_ref[a : a + 1, :]
        )


def passed_along(block, axis, distance):
    devices = range(lax.axis_size(axis))
    route = [((i - distance) % len(devices), i) for i in devices]
    return lax.ppermute(block, axis, route)


def routed(block, axis, source):
    return lax.ppermute(block, axis, [(source(i), i) for i in range(lax.axis_size(axis))])


def near_pair(block):
    return routed(block, "dom", lambda i: i ^ 1)


def far_pair(block):
    return routed(block, "dom", lambda i: (i - 1 + i % 2 * 2) % lax.axis_size("dom"))


def across(block):
    beads = lax.axis_size("bead")
    route = [(i ^ (2 * beads + 4), i) for i in range(beads * lax.axis_size("dom"))]
    return lax.ppermute(block, ("dom", "bead"), route)


def after(value, *others):
    return lax.optimization_barrier((value, others))[0]


def matrix_part(points, point_weights):
    dom = lax.axis_index("dom")
    which, height = dom % 2, points.shape[2] // 4
    p = lax.dynamic_index_in_dim(points, which, 0, keepdims=False).astype(F32)
    w = lax.dynamic_index_in_dim(point_weights, which, 0, keepdims=False).astype(F32)
    left = lax.dynamic_slice_in_dim(p, dom // 4 * height, height, axis=1)
    return lax.dot_general(
        left * (2.0 * w)[:, None],
        p,
        (((0,), (0,)), ((), ())),
        precision=lax.Precision.HIGHEST,
        preferred_element_type=F32,
    )


def add_kernel(part_ref, other_ref, *outs):
    total = part_ref[...] + other_ref[...].astype(F32)
    for out in outs:
        out[...] = total.astype(out.dtype)


def ring_kernel(*refs):
    *pieces, out_ref = refs
    rows = pieces[0].shape[0]
    height = lax.axis_index("dom") // 4
    for k, piece in enumerate(pieces):
        place = (height + 4 - k) % 4
        out_ref[pl.ds(pl.multiple_of(place * rows, rows), rows), :] = piece[...]


def shards(
    positions,
    velocities,
    species,
    neighbours,
    neighbour_count,
    send_lists,
    projection,
    phase_shift,
    points,
    point_weights,
):
    own, sent = positions.shape[2], send_lists.shape[1]
    ghosts = 2 * sent
    everyone = own + ghosts
    features = points.shape[2]
    shape = jax.ShapeDtypeStruct
    species = species.reshape(1, own)
    position, velocity = positions.transpose(1, 0, 2), velocities.transpose(1, 0, 2)
    projection = projection.transpose(1, 0, 2)
    sends = (shape((4, sent), F32),) * 2
    wide = pltpu.VMEM((LANES, own), F32)
    slab = (features // 4, features)
    counts = neighbour_count.reshape(1, own)

    def count(part):
        return call(
            functools.partial(count_kernel, part),
            shape((ghosts, own), F32),
            [pltpu.VMEM((NEIGH, own), F32)],
        )(neighbours, counts)

    own_call = call(
        own_kernel,
        (
            shape((own, LANES), F32),
            shape((own, 4 * features), BF16),
            shape((own, 4 * features), F32),
        ),
        [wide],
        LIMIT,
    )
    weigh_call = call(
        weigh_kernel,
        (
            shape((ghosts, LANES), F32),
            shape((everyone, own), F32),
            shape((own, everyone), BF16),
            shape((ghosts, 4 * features), BF16),
        ),
        [pltpu.VMEM((LANES, ghosts), F32)],
        LIMIT,
    )
    describe_call = call(
        describe_kernel,
        (shape((own, 2 * features), F32), shape((own, features), BF16)),
        [pltpu.VMEM((own, 4 * FB), F32)],
        LIMIT,
    )
    ghost_force_call = call(
        ghost_force_kernel,
        (
            shape((own, features), F32),
            shape((own, 4 * features), BF16),
            shape((3, own), F32),
            shape((3, sent), F32),
            shape((3, sent), F32),
        ),
        [
            pltpu.VMEM((ghosts, 4 * FB), F32),
            pltpu.VMEM((ghosts, own), F32),
            pltpu.VMEM((3, ghosts, LANES), F32),
        ],
        LIMIT,
    )
    own_force_call = call(
        own_force_kernel,
        shape((3, own), F32),
        [
            pltpu.VMEM((own, 4 * FB), F32),
            pltpu.VMEM((own, own), F32),
            pltpu.VMEM((3, own, LANES), F32),
        ],
        LIMIT,
    )

    to_near, to_far = call(first_kernel, sends, [wide])(position, species, send_lists)
    part = matrix_part(points, point_weights)
    sent_part = part.astype(BF16)
    for step in range(STEPS):
        last = step == STEPS - 1
        if step == 0:
            other = across(sent_part)
            number = [count(k) for k in range(3)]
            part, held = call(add_kernel, (shape(slab, F32), shape(slab, BF16)))(
                part, after(other, to_far, to_near, *number)
            )
            other = routed(held, "bead", lambda i: i ^ 1)
            to_far, to_near = after(to_far, held), after(to_near, held)
        from_far = far_pair(to_far)
        from_near = near_pair(to_near)
        start = after(position, held) if step == 0 else position
        cols, waves, turned = own_call(start, species, projection, phase_shift)
        if step == 0:
            part, held = call(add_kernel, (shape(slab, F32), shape(slab, BF16)))(
                part, after(other, cols, from_far, from_near)
            )
            other = routed(held, "bead", lambda i: i ^ 3)
            above = passed_along(after(position, held), "bead", -1)
            state = weigh_call(
                after(position, held), from_near, from_far, cols, projection, *number
            )
            ghost_cols, weight, weight_turned, ghost_waves = state
            held = call(add_kernel, (shape(slab, BF16),))(part, after(other, above, *state))[0]
            pieces = [held] + [routed(held, "dom", lambda i: (i - 4 * k) % 16) for k in (1, 2, 3)]
            sines, low = describe_call(after(weight_turned, held), waves, ghost_waves, turned)
            half = call(ring_kernel, shape((features, features), BF16))(
                pieces[0], *[after(piece, low) for piece in pieces[1:]]
            )
            other_half = near_pair(half)
            below = passed_along(after(position, half), "bead", 1)
        else:
            above = passed_along(after(position, cols, from_far, from_near), "bead", -1)
            ghost_cols, weight, weight_turned, ghost_waves = weigh_call(
                position, from_near, from_far, cols, projection, *number
            )
            sines, low = describe_call(weight_turned, waves, ghost_waves, turned)
            below = passed_along(after(position, low), "bead", 1)
        grad, spread, centre, near_force, far_force = ghost_force_call(
            low,
            half,
            other_half,
            cols,
            turned,
            weight,
            ghost_waves,
            ghost_cols,
            position,
            projection,
        )
        far_back = far_pair(far_force)
        near_back = near_pair(near_force)
        force = own_force_call(
            grad, spread, sines, waves, weight, cols, position, centre, projection
        )
        moved = shape(position.shape, F32)
        position, velocity, *rest = call(
            functools.partial(update_kernel, last),
            (moved, moved) + (() if last else sends),
            [pltpu.VMEM((LANES, sent), F32), wide],
        )(
            force,
            near_back,
            far_back,
            send_lists,
            position,
            velocity,
            below,
            above,
            species,
        )
        if not last:
            to_near, to_far = rest
    return (position.transpose(1, 0, 2), velocity.transpose(1, 0, 2))


def solution(mesh):
    placed = (
        P("bead", None, "dom"),
        P("bead", None, "dom"),
        P("dom"),
        P(None, "dom"),
        P("dom"),
        P(None, "dom"),
        P(),
        P(),
        P(None, "bead", None),
        P(None, "bead"),
    )
    return jax.shard_map(
        shards,
        mesh=mesh,
        in_specs=placed,
        out_specs=(P("bead", None, "dom"), P("bead", None, "dom")),
        check_vma=False,
    )
```

```python
import functools

import jax
import jax.numpy as jnp
from jax import lax
from jax.experimental import pallas as pl
from jax.experimental.pallas import tpu as pltpu
from jax.sharding import PartitionSpec as P

NEIGH = 32
STEPS = 2

WIDTH = 1.5
DT = 0.1
KAPPA = 0.5

F32, BF16 = jnp.float32, jnp.bfloat16
LANES = 128
ROWS = 32
FB = 256
TURN = 0.15915494309189535
SIN = (3.1415927410125732, -5.167710304260254, 2.550077438354492, -0.5982903838157654, 0.07765591144561768)
COS = (0.9999999403953552, -4.934792995452881, 4.05841064453125, -1.3318729400634766, 0.21968242526054382)
VMEM = pl.BlockSpec(memory_space=pltpu.VMEM)
MIB = 1024 * 1024
LIMIT = 16


def call(body, outs, scratch=(), limit=8):
    return pl.pallas_call(
        body,
        out_shape=outs,
        out_specs=jax.tree.map(lambda _: VMEM, outs),
        scratch_shapes=scratch,
        compiler_params=pltpu.CompilerParams(vmem_limit_bytes=limit * MIB),
    )


def cos_sin(turns):
    f = turns - jnp.round(turns)
    g = f * f
    s, c = SIN[-1], COS[-1]
    for low in SIN[-2::-1]:
        s = s * g + low
    for low in COS[-2::-1]:
        c = c * g + low
    s = s * f
    twice = s + s
    return 1.0 - twice * s, twice * c


def core_of():
    return lax.axis_index("dom") % 2


def count_kernel(part, neighbours_ref, count_ref, number_ref, named):
    rows, atoms = number_ref.shape
    slot = lax.broadcasted_iota(jnp.int32, neighbours_ref.shape, 0)
    row = jnp.where(slot < count_ref[...], neighbours_ref[...] - part * rows, -1)
    if part * rows >= atoms:
        swapped = jnp.where(row >= rows // 2, row - rows // 2, row + rows // 2)
        row = jnp.where((core_of() == 0) & (row >= 0), swapped, row)
    named[...] = jnp.where((row >= 0) & (row < rows), row, -1).astype(F32)
    one, zero = jnp.ones((), BF16), jnp.zeros((), BF16)
    step = 2 * ROWS
    for start in range(0, rows, step):
        local = (lax.broadcasted_iota(jnp.int32, (step, atoms), 0) + start).astype(F32).astype(BF16)
        total = jnp.zeros((step, atoms), BF16)
        for k in range(NEIGH):
            total = total + jnp.where(local == named[k : k + 1, :].astype(BF16), one, zero)
        number_ref[start : start + step, :] = total.astype(F32)


def near_far_lists(lists_ref):
    core = core_of()
    return [lists_ref[pl.ds(1 - core, 1), :], lists_ref[pl.ds(core, 1), :]]


def gather_rows(columns, list_row, count):
    atoms, listed = columns.shape[0], list_row.shape[1]
    hit = lax.broadcasted_iota(jnp.int32, (atoms, listed), 0) == list_row
    return [
        jnp.sum(jnp.where(hit, columns[:, a : a + 1], 0.0), axis=0, keepdims=True)
        for a in range(count)
    ]


def send_rows(position_rows, species_row, lists, near_ref, far_ref, wide):
    wide[...] = jnp.zeros_like(wide)
    for a in range(3):
        wide[a : a + 1, :] = position_rows[a]
    wide[3:4, :] = species_row
    columns = wide[...].T
    for out, listed in zip((near_ref, far_ref), lists):
        for a, row in enumerate(gather_rows(columns, listed, 4)):
            out[a : a + 1, :] = row


def first_kernel(position_ref, species_ref, lists_ref, near_ref, far_ref, wide):
    rows = [position_ref[a] for a in range(3)]
    lists = near_far_lists(lists_ref)
    send_rows(rows, species_ref[...].astype(F32), lists, near_ref, far_ref, wide)


def update_kernel(
    last,
    force_ref,
    near_back_ref,
    far_back_ref,
    lists_ref,
    position_ref,
    velocity_ref,
    below_ref,
    above_ref,
    species_ref,
    new_position_ref,
    new_velocity_ref,
    *rest,
):
    atoms = position_ref.shape[2]
    listed = lists_ref.shape[1]
    wide = rest[-1]
    back = rest[-2]
    lists = near_far_lists(lists_ref)
    extra = [0.0, 0.0, 0.0]
    for names, ref in zip(lists, (near_back_ref, far_back_ref)):
        back[...] = jnp.zeros_like(back)
        back[0:3, :] = ref[...]
        back[3:4, :] = names.astype(F32)
        values = back[...].T
        hit = lax.broadcasted_iota(jnp.int32, (listed, atoms), 1).astype(F32) == values[:, 3:4]
        for a in range(3):
            extra[a] = extra[a] + jnp.sum(
                jnp.where(hit, values[:, a : a + 1], 0.0), axis=0, keepdims=True
            )
    species = species_ref[...]
    mass = jnp.where(species == 0, 16.0, 1.0)
    rows = []
    for a in range(3):
        here = position_ref[a]
        chain = 2.0 * here - below_ref[a] - above_ref[a]
        total = force_ref[a : a + 1, :] + extra[a] - KAPPA * mass * chain
        velocity = velocity_ref[a] + DT * (total / mass)
        place = here + DT * velocity
        new_velocity_ref[a] = velocity
        new_position_ref[a] = place
        rows.append(place)
    if not last:
        send_rows(rows, species.astype(F32), lists, rest[0], rest[1], wide)


def each(count, body, carry=0):
    for c in range(count // ROWS):
        carry = body(c, carry)
    return carry


def chunk_rows(c, first=0):
    return slice(first + c * ROWS, first + (c + 1) * ROWS)


def own_kernel(
    position_ref,
    species_ref,
    projection_ref,
    shift_ref,
    cols,
    waves,
    turned,
    rows_in,
):
    own = position_ref.shape[2]
    features = projection_ref.shape[2]
    rows_in[...] = jnp.zeros_like(rows_in)
    for a in range(3):
        rows_in[a : a + 1, :] = position_ref[a]
    rows_in[3:4, :] = species_ref[...].astype(F32)
    cols[...] = rows_in[...].T

    shift_cos, shift_sin = cos_sin(shift_ref[...] * TURN)
    for block in range(features // FB):
        mine = slice(block * FB, (block + 1) * FB)
        base = block * 4 * FB
        wave = [
            [projection_ref[a, s : s + 1, mine] * TURN for a in range(3)] for s in range(2)
        ]
        turn_cos = [shift_cos[s : s + 1, mine] for s in range(2)]
        turn_sin = [shift_sin[s : s + 1, mine] for s in range(2)]

        def own_waves(c, carry):
            rows = chunk_rows(c)
            there = cols[rows, :]
            x, y, z = (jnp.broadcast_to(there[:, a : a + 1], (ROWS, FB)) for a in range(3))
            second = jnp.broadcast_to(there[:, 3:4], (ROWS, FB)) > 0.5
            for s in range(2):
                cos, sin = cos_sin(x * wave[s][0] + y * wave[s][1] + z * wave[s][2])
                at = base + s * 2 * FB
                turned[rows, at : at + FB] = turn_cos[s] * cos + turn_sin[s] * sin
                turned[rows, at + FB : at + 2 * FB] = turn_sin[s] * cos - turn_cos[s] * sin
                if s == 0:
                    cos, sin = jnp.where(second, 0.0, cos), jnp.where(second, 0.0, sin)
                else:
                    cos, sin = jnp.where(second, cos, 0.0), jnp.where(second, sin, 0.0)
                waves[rows, at : at + FB] = cos.astype(BF16)
                waves[rows, at + FB : at + 2 * FB] = sin.astype(BF16)
            return carry

        each(own, own_waves)


def weigh_kernel(
    position_ref,
    near_ref,
    far_ref,
    own_cols,
    projection_ref,
    *rest,
):
    *numbers, ghost_cols, weight, weight_turned, waves, rows_in = rest
    own = position_ref.shape[2]
    sent = near_ref.shape[1]
    features = projection_ref.shape[2]

    rows_in[...] = jnp.zeros_like(rows_in)
    rows_in[0:4, 0:sent] = near_ref[...]
    rows_in[0:4, sent : 2 * sent] = far_ref[...]
    ghost_cols[...] = rows_in[...].T
    here = [position_ref[a] for a in range(3)]

    for k, number_ref in enumerate(numbers):
        first = k * number_ref.shape[0]
        cols, skip = (own_cols, first) if first < own else (ghost_cols, first - own)

        def weigh(c, carry):
            there = cols[chunk_rows(c, skip), :]
            square = 0.0
            for a in range(3):
                d = there[:, a : a + 1] - here[a]
                square = square + d * d
            weight[chunk_rows(c, first), :] = number_ref[chunk_rows(c), :] * jnp.exp(
                square * (-1.0 / (2.0 * WIDTH * WIDTH))
            )
            return carry

        each(number_ref.shape[0], weigh)
    weight_turned[...] = weight[...].T.astype(BF16)

    for block in range(features // FB):
        mine = slice(block * FB, (block + 1) * FB)
        base = block * 4 * FB
        wave = [
            [projection_ref[a, s : s + 1, mine] * TURN for a in range(3)] for s in range(2)
        ]

        def ghost_waves(c, carry):
            rows = chunk_rows(c)
            there = ghost_cols[rows, :]
            x, y, z = (jnp.broadcast_to(there[:, a : a + 1], (ROWS, FB)) for a in range(3))
            second = jnp.broadcast_to(there[:, 3:4], (ROWS, FB)) > 0.5
            px, py, pz = (jnp.where(second, wave[1][a], wave[0][a]) for a in range(3))
            cos, sin = cos_sin(x * px + y * py + z * pz)
            for s in range(2):
                at = base + s * 2 * FB
                for k, part in enumerate((cos, sin)):
                    if s == 0:
                        part = jnp.where(second, 0.0, part)
                    else:
                        part = jnp.where(second, part, 0.0)
                    waves[rows, at + k * FB : at + (k + 1) * FB] = part.astype(BF16)
            return carry

        each(2 * sent, ghost_waves)


def describe_kernel(
    weight_turned,
    own_waves,
    ghost_waves,
    turned,
    sines,
    low,
    sums,
):
    own = weight_turned.shape[0]
    features = low.shape[1]
    for block in range(features // FB):
        mine = slice(block * FB, (block + 1) * FB)
        base = block * 4 * FB
        sums[...] = jnp.dot(
            weight_turned[:, 0:own], own_waves[:, base : base + 4 * FB], preferred_element_type=F32
        ) + jnp.dot(
            weight_turned[:, own:], ghost_waves[:, base : base + 4 * FB], preferred_element_type=F32
        )

        def describe(c, carry):
            rows = chunk_rows(c)
            total = 0.0
            for s in range(2):
                at = base + s * 2 * FB
                tr, ti = turned[rows, at : at + FB], turned[rows, at + FB : at + 2 * FB]
                ur = sums[rows, s * 2 * FB : s * 2 * FB + FB]
                ui = sums[rows, s * 2 * FB + FB : s * 2 * FB + 2 * FB]
                total = total + (tr * ur - ti * ui)
                first = s * features + block * FB
                sines[rows, first : first + FB] = tr * ui + ti * ur
            low[rows, mine] = total.astype(BF16)
            return carry

        each(own, describe)


def fold(value):
    total = value[:, 0:LANES]
    for k in range(1, value.shape[1] // LANES):
        total = total + value[:, k * LANES : (k + 1) * LANES]
    return total


def pull_rows(first, cols, waves, weight, spread, projection_ref, here, parts, back, product):
    count = cols.shape[0]
    features = projection_ref.shape[2]
    held = weight[first : first + count, :].astype(BF16)
    for block in range(features // FB):
        mine = slice(block * FB, (block + 1) * FB)
        base = block * 4 * FB
        raw = [[projection_ref[a, s : s + 1, mine] for a in range(3)] for s in range(2)]
        back[...] = jnp.dot(held, spread[:, base : base + 4 * FB], preferred_element_type=F32)

        def pull(c, carry):
            rows = chunk_rows(c)
            second = jnp.broadcast_to(cols[rows, 3:4], (ROWS, FB)) > 0.5
            total = 0.0
            for s in range(2):
                at = base + s * 2 * FB
                er = waves[rows, at : at + FB].astype(F32)
                ei = waves[rows, at + FB : at + 2 * FB].astype(F32)
                vr = back[rows, s * 2 * FB : s * 2 * FB + FB]
                vi = back[rows, s * 2 * FB + FB : s * 2 * FB + 2 * FB]
                total = total + (ei * vr - er * vi)
            for a in range(3):
                coeff = jnp.where(second, raw[1][a], raw[0][a])
                parts[a, rows, :] = parts[a, rows, :] + fold(total * coeff)
            return carry

        each(count, pull)

    product[...] = lax.dot_general(
        waves[...], spread[...], (((1,), (1,)), ((), ())), preferred_element_type=F32
    )

    def along(c, carry):
        rows = chunk_rows(c)
        there = cols[rows, :]
        z = weight[chunk_rows(c, first), :] * product[rows, :] * (1.0 / (WIDTH * WIDTH))
        out = []
        for a in range(3):
            pull_a = z * (there[:, a : a + 1] - here[a])
            parts[a, rows, :] = parts[a, rows, :] + fold(pull_a)
            total = pull_a[0:8]
            for k in range(1, ROWS // 8):
                total = total + pull_a[8 * k : 8 * k + 8]
            out.append(carry[a] + total)
        return tuple(out)

    start = tuple(jnp.zeros((8, here[0].shape[1]), F32) for _ in range(3))
    return each(count, along, carry=start)


def ghost_force_kernel(
    low,
    half_ref,
    other_ref,
    own_cols,
    turned,
    weight,
    waves,
    cols,
    position_ref,
    projection_ref,
    grad,
    spread,
    centre_ref,
    near_ref,
    far_ref,
    back,
    product,
    parts,
):
    own, features = grad.shape
    sent = near_ref.shape[1]
    here = [position_ref[a] for a in range(3)]
    mine_is = core_of().astype(F32)
    grad[...] = jnp.where(
        own_cols[:, 3:4] == mine_is,
        jnp.dot(low[...], half_ref[...], preferred_element_type=F32),
        jnp.dot(low[...], other_ref[...], preferred_element_type=F32),
    )
    for block in range(features // FB):
        mine = slice(block * FB, (block + 1) * FB)
        base = block * 4 * FB

        def spread_out(c, carry):
            rows = chunk_rows(c)
            g = grad[rows, mine]
            for s in range(2):
                at = base + s * 2 * FB
                spread[rows, at : at + FB] = (g * turned[rows, at : at + FB]).astype(BF16)
                spread[rows, at + FB : at + 2 * FB] = (
                    -g * turned[rows, at + FB : at + 2 * FB]
                ).astype(BF16)
            return carry

        each(own, spread_out)

    parts[...] = jnp.zeros_like(parts)
    centre = pull_rows(
        own, cols, waves, weight, spread, projection_ref, here, parts, back, product
    )
    for a in range(3):
        row = jnp.sum(parts[a].T, axis=0, keepdims=True)
        centre_ref[a : a + 1, :] = jnp.sum(centre[a], axis=0, keepdims=True)
        near_ref[a : a + 1, :] = row[:, 0:sent]
        far_ref[a : a + 1, :] = row[:, sent:]


def own_force_kernel(
    grad,
    spread,
    sines,
    waves,
    weight,
    cols,
    position_ref,
    centre_ref,
    projection_ref,
    force_ref,
    back,
    product,
    parts,
):
    own, features = grad.shape
    here = [position_ref[a] for a in range(3)]
    raw = [[projection_ref[a, s : s + 1, :] for a in range(3)] for s in range(2)]

    def turn(c, carry):
        rows = chunk_rows(c)
        g = grad[rows, :]
        t0 = g * sines[rows, 0:features]
        t1 = g * sines[rows, features : 2 * features]
        for a in range(3):
            parts[a, rows, :] = -fold(t0 * raw[0][a] + t1 * raw[1][a])
        return carry

    each(own, turn)
    centre = pull_rows(
        0, cols, waves, weight, spread, projection_ref, here, parts, back, product
    )
    for a in range(3):
        row = jnp.sum(parts[a].T, axis=0, keepdims=True)
        force_ref[a : a + 1, :] = (
            row - jnp.sum(centre[a], axis=0, keepdims=True) - centre_ref[a : a + 1, :]
        )


def passed_along(block, axis, distance):
    devices = range(lax.axis_size(axis))
    route = [((i - distance) % len(devices), i) for i in devices]
    return lax.ppermute(block, axis, route)


def routed(block, axis, source):
    return lax.ppermute(block, axis, [(source(i), i) for i in range(lax.axis_size(axis))])


def near_pair(block):
    return routed(block, "dom", lambda i: i ^ 1)


def far_pair(block):
    return routed(block, "dom", lambda i: (i - 1 + i % 2 * 2) % lax.axis_size("dom"))


def across(block):
    beads = lax.axis_size("bead")
    route = [(i ^ (2 * beads + 4), i) for i in range(beads * lax.axis_size("dom"))]
    return lax.ppermute(block, ("dom", "bead"), route)


def after(value, *others):
    return lax.optimization_barrier((value, others))[0]


def matrix_part(points, point_weights):
    dom = lax.axis_index("dom")
    which, height = dom % 2, points.shape[2] // 4
    p = lax.dynamic_index_in_dim(points, which, 0, keepdims=False).astype(F32)
    w = lax.dynamic_index_in_dim(point_weights, which, 0, keepdims=False).astype(F32)
    left = lax.dynamic_slice_in_dim(p, dom // 4 * height, height, axis=1)
    return lax.dot_general(
        left * (2.0 * w)[:, None],
        p,
        (((0,), (0,)), ((), ())),
        precision=lax.Precision.HIGHEST,
        preferred_element_type=F32,
    )


def add_kernel(part_ref, other_ref, *outs):
    total = part_ref[...] + other_ref[...].astype(F32)
    for out in outs:
        out[...] = total.astype(out.dtype)


def block_at(k):
    width = 128
    return pl.ds(pl.multiple_of(k % 4 * width, width), width)


def cut_kernel(part_ref, *outs):
    height = lax.axis_index("dom") // 4
    for j in range(3):
        block = part_ref[:, block_at(height + j)]
        for out in outs:
            out[:, j * LANES : (j + 1) * LANES] = block.astype(out.dtype)


def ring_kernel(*refs):
    *pieces, out_ref = refs
    height = lax.axis_index("dom") // 4
    for k, piece in enumerate(pieces):
        row = height + 4 - k
        for j in range(3):
            out_ref[block_at(row), block_at(row + j)] = piece[:, j * LANES : (j + 1) * LANES]
        turned = piece[:, LANES : 2 * LANES].astype(F32).T.astype(BF16)
        out_ref[block_at(row + 1), block_at(row)] = turned


def shards(
    positions,
    velocities,
    species,
    neighbours,
    neighbour_count,
    send_lists,
    projection,
    phase_shift,
    points,
    point_weights,
):
    own, sent = positions.shape[2], send_lists.shape[1]
    ghosts = 2 * sent
    everyone = own + ghosts
    features = points.shape[2]
    shape = jax.ShapeDtypeStruct
    species = species.reshape(1, own)
    position, velocity = positions.transpose(1, 0, 2), velocities.transpose(1, 0, 2)
    projection = projection.transpose(1, 0, 2)
    sends = (shape((4, sent), F32),) * 2
    wide = pltpu.VMEM((LANES, own), F32)
    slab = (features // 4, features // 4 * 3)
    counts = neighbour_count.reshape(1, own)

    def count(part):
        return call(
            functools.partial(count_kernel, part),
            shape((ghosts, own), F32),
            [pltpu.VMEM((NEIGH, own), F32)],
        )(neighbours, counts)

    own_call = call(
        own_kernel,
        (
            shape((own, LANES), F32),
            shape((own, 4 * features), BF16),
            shape((own, 4 * features), F32),
        ),
        [wide],
        LIMIT,
    )
    weigh_call = call(
        weigh_kernel,
        (
            shape((ghosts, LANES), F32),
            shape((everyone, own), F32),
            shape((own, everyone), BF16),
            shape((ghosts, 4 * features), BF16),
        ),
        [pltpu.VMEM((LANES, ghosts), F32)],
        LIMIT,
    )
    describe_call = call(
        describe_kernel,
        (shape((own, 2 * features), F32), shape((own, features), BF16)),
        [pltpu.VMEM((own, 4 * FB), F32)],
        LIMIT,
    )
    ghost_force_call = call(
        ghost_force_kernel,
        (
            shape((own, features), F32),
            shape((own, 4 * features), BF16),
            shape((3, own), F32),
            shape((3, sent), F32),
            shape((3, sent), F32),
        ),
        [
            pltpu.VMEM((ghosts, 4 * FB), F32),
            pltpu.VMEM((ghosts, own), F32),
            pltpu.VMEM((3, ghosts, LANES), F32),
        ],
        LIMIT,
    )
    own_force_call = call(
        own_force_kernel,
        shape((3, own), F32),
        [
            pltpu.VMEM((own, 4 * FB), F32),
            pltpu.VMEM((own, own), F32),
            pltpu.VMEM((3, own, LANES), F32),
        ],
        LIMIT,
    )

    to_near, to_far = call(first_kernel, sends, [wide])(position, species, send_lists)
    part, sent_part = call(cut_kernel, (shape(slab, F32), shape(slab, BF16)))(
        matrix_part(points, point_weights)
    )
    for step in range(STEPS):
        last = step == STEPS - 1
        if step == 0:
            other = across(sent_part)
            number = [count(k) for k in range(3)]
            part, held = call(add_kernel, (shape(slab, F32), shape(slab, BF16)))(
                part, after(other, to_far, to_near, *number)
            )
            other = routed(held, "bead", lambda i: i ^ 1)
            to_far, to_near = after(to_far, held), after(to_near, held)
        from_far = far_pair(to_far)
        from_near = near_pair(to_near)
        start = after(position, held) if step == 0 else position
        cols, waves, turned = own_call(start, species, projection, phase_shift)
        if step == 0:
            part, held = call(add_kernel, (shape(slab, F32), shape(slab, BF16)))(
                part, after(other, cols, from_far, from_near)
            )
            other = routed(held, "bead", lambda i: i ^ 3)
            state = weigh_call(
                after(position, held), from_near, from_far, cols, projection, *number
            )
            ghost_cols, weight, weight_turned, ghost_waves = state
            held = call(add_kernel, (shape(slab, BF16),))(part, after(other, *state))[0]
            pieces = [held] + [routed(held, "dom", lambda i: (i - 4 * k) % 16) for k in (1, 2, 3)]
            above = passed_along(after(position, held), "bead", -1)
            sines, low = describe_call(after(weight_turned, held), waves, ghost_waves, turned)
            half = call(ring_kernel, shape((features, features), BF16))(
                pieces[0], *[after(piece, low, above) for piece in pieces[1:]]
            )
            other_half = near_pair(half)
            below = passed_along(after(position, half), "bead", 1)
        else:
            above = passed_along(after(position, cols, from_far, from_near), "bead", -1)
            ghost_cols, weight, weight_turned, ghost_waves = weigh_call(
                position, from_near, from_far, cols, projection, *number
            )
            sines, low = describe_call(weight_turned, waves, ghost_waves, turned)
            below = passed_along(after(position, low), "bead", 1)
        grad, spread, centre, near_force, far_force = ghost_force_call(
            low,
            half,
            other_half,
            cols,
            turned,
            weight,
            ghost_waves,
            ghost_cols,
            position,
            projection,
        )
        far_back = far_pair(far_force)
        near_back = near_pair(near_force)
        force = own_force_call(
            grad, spread, sines, waves, weight, cols, position, centre, projection
        )
        moved = shape(position.shape, F32)
        position, velocity, *rest = call(
            functools.partial(update_kernel, last),
            (moved, moved) + (() if last else sends),
            [pltpu.VMEM((LANES, sent), F32), wide],
        )(
            force,
            near_back,
            far_back,
            send_lists,
            position,
            velocity,
            below,
            above,
            species,
        )
        if not last:
            to_near, to_far = rest
    return (position.transpose(1, 0, 2), velocity.transpose(1, 0, 2))


def solution(mesh):
    placed = (
        P("bead", None, "dom"),
        P("bead", None, "dom"),
        P("dom"),
        P(None, "dom"),
        P("dom"),
        P(None, "dom"),
        P(),
        P(),
        P(None, "bead", None),
        P(None, "bead"),
    )
    return jax.shard_map(
        shards,
        mesh=mesh,
        in_specs=placed,
        out_specs=(P("bead", None, "dom"), P("bead", None, "dom")),
        check_vma=False,
    )
```

```python
import functools

import jax
import jax.numpy as jnp
from jax import lax
from jax.experimental import pallas as pl
from jax.experimental.pallas import tpu as pltpu
from jax.sharding import PartitionSpec as P

NEIGH = 32
STEPS = 2

WIDTH = 1.5
DT = 0.1
KAPPA = 0.5

F32, BF16 = jnp.float32, jnp.bfloat16
LANES = 128
PACKED = 16
ROWS = 32
FB = 256
TURN = 0.15915494309189535
SIN = (3.1415927410125732, -5.167710304260254, 2.550077438354492, -0.5982903838157654, 0.07765591144561768)
COS = (0.9999999403953552, -4.934792995452881, 4.05841064453125, -1.3318729400634766, 0.21968242526054382)
VMEM = pl.BlockSpec(memory_space=pltpu.VMEM)
MIB = 1024 * 1024
LIMIT = 16


def call(body, outs, scratch=(), limit=8):
    return pl.pallas_call(
        body,
        out_shape=outs,
        out_specs=jax.tree.map(lambda _: VMEM, outs),
        scratch_shapes=scratch,
        compiler_params=pltpu.CompilerParams(vmem_limit_bytes=limit * MIB),
    )


def cos_sin(turns):
    f = turns - jnp.round(turns)
    g = f * f
    s, c = SIN[-1], COS[-1]
    for low in SIN[-2::-1]:
        s = s * g + low
    for low in COS[-2::-1]:
        c = c * g + low
    s = s * f
    twice = s + s
    return 1.0 - twice * s, twice * c


def core_of():
    return lax.axis_index("dom") % 2


def count_kernel(part, neighbours_ref, count_ref, number_ref, named):
    rows, atoms = number_ref.shape
    slot = lax.broadcasted_iota(jnp.int32, neighbours_ref.shape, 0)
    row = jnp.where(slot < count_ref[...], neighbours_ref[...] - part * rows, -1)
    if part * rows >= atoms:
        swapped = jnp.where(row >= rows // 2, row - rows // 2, row + rows // 2)
        row = jnp.where((core_of() == 0) & (row >= 0), swapped, row)
    named[...] = jnp.where((row >= 0) & (row < rows), row, -1).astype(F32)
    one, zero = jnp.ones((), BF16), jnp.zeros((), BF16)
    step = 2 * ROWS
    for start in range(0, rows, step):
        local = (lax.broadcasted_iota(jnp.int32, (step, atoms), 0) + start).astype(F32).astype(BF16)
        total = jnp.zeros((step, atoms), BF16)
        for k in range(NEIGH):
            total = total + jnp.where(local == named[k : k + 1, :].astype(BF16), one, zero)
        number_ref[start : start + step, :] = total.astype(F32)


def near_far_lists(lists_ref):
    core = core_of()
    return [lists_ref[pl.ds(1 - core, 1), :], lists_ref[pl.ds(core, 1), :]]


def gather_rows(columns, list_row, count):
    atoms, listed = columns.shape[0], list_row.shape[1]
    hit = lax.broadcasted_iota(jnp.int32, (atoms, listed), 0) == list_row
    return [
        jnp.sum(jnp.where(hit, columns[:, a : a + 1], 0.0), axis=0, keepdims=True)
        for a in range(count)
    ]


def send_rows(position_rows, species_row, lists, near_ref, far_ref, wide):
    wide[...] = jnp.zeros_like(wide)
    for a in range(3):
        wide[a : a + 1, :] = position_rows[a]
    wide[3:4, :] = species_row
    columns = wide[...].T
    for out, listed in zip((near_ref, far_ref), lists):
        for a, row in enumerate(gather_rows(columns, listed, 4)):
            out[a : a + 1, :] = row


def first_kernel(position_ref, species_ref, lists_ref, near_ref, far_ref, wide):
    rows = [position_ref[a] for a in range(3)]
    lists = near_far_lists(lists_ref)
    send_rows(rows, species_ref[...].astype(F32), lists, near_ref, far_ref, wide)


def update_kernel(
    last,
    force_ref,
    near_back_ref,
    far_back_ref,
    lists_ref,
    position_ref,
    velocity_ref,
    one_bead_ref,
    other_bead_ref,
    species_ref,
    new_position_ref,
    new_velocity_ref,
    *rest,
):
    atoms = position_ref.shape[2]
    listed = lists_ref.shape[1]
    wide = rest[-1]
    back = rest[-2]
    lists = near_far_lists(lists_ref)
    extra = [0.0, 0.0, 0.0]
    for names, ref in zip(lists, (near_back_ref, far_back_ref)):
        back[...] = jnp.zeros_like(back)
        back[0:3, :] = ref[...]
        back[3:4, :] = names.astype(F32)
        values = back[...].T
        hit = lax.broadcasted_iota(jnp.int32, (listed, atoms), 1).astype(F32) == values[:, 3:4]
        for a in range(3):
            extra[a] = extra[a] + jnp.sum(
                jnp.where(hit, values[:, a : a + 1], 0.0), axis=0, keepdims=True
            )
    species = species_ref[...]
    mass = jnp.where(species == 0, 16.0, 1.0)
    rows = []
    for a in range(3):
        here = position_ref[a]
        chain = 2.0 * here - one_bead_ref[a] - other_bead_ref[a]
        total = force_ref[a : a + 1, :] + extra[a] - KAPPA * mass * chain
        velocity = velocity_ref[a] + DT * (total / mass)
        place = here + DT * velocity
        new_velocity_ref[a] = velocity
        new_position_ref[a] = place
        rows.append(place)
    if not last:
        send_rows(rows, species.astype(F32), lists, rest[0], rest[1], wide)


def each(count, body, carry=0):
    for c in range(count // ROWS):
        carry = body(c, carry)
    return carry


def chunk_rows(c, first=0):
    return slice(first + c * ROWS, first + (c + 1) * ROWS)


def own_kernel(
    position_ref,
    species_ref,
    projection_ref,
    shift_ref,
    cols,
    waves,
    turned,
    rows_in,
):
    own = position_ref.shape[2]
    features = projection_ref.shape[2]
    rows_in[...] = jnp.zeros_like(rows_in)
    for a in range(3):
        rows_in[a : a + 1, :] = position_ref[a]
    rows_in[3:4, :] = species_ref[...].astype(F32)
    cols[...] = rows_in[...].T

    shift_cos, shift_sin = cos_sin(shift_ref[...] * TURN)
    for block in range(features // FB):
        mine = slice(block * FB, (block + 1) * FB)
        base = block * 4 * FB
        wave = [
            [projection_ref[a, s : s + 1, mine] * TURN for a in range(3)] for s in range(2)
        ]
        turn_cos = [shift_cos[s : s + 1, mine] for s in range(2)]
        turn_sin = [shift_sin[s : s + 1, mine] for s in range(2)]

        def own_waves(c, carry):
            rows = chunk_rows(c)
            there = cols[rows, :]
            x, y, z = (jnp.broadcast_to(there[:, a : a + 1], (ROWS, FB)) for a in range(3))
            second = jnp.broadcast_to(there[:, 3:4], (ROWS, FB)) > 0.5
            for s in range(2):
                cos, sin = cos_sin(x * wave[s][0] + y * wave[s][1] + z * wave[s][2])
                at = base + s * 2 * FB
                turned[rows, at : at + FB] = turn_cos[s] * cos + turn_sin[s] * sin
                turned[rows, at + FB : at + 2 * FB] = turn_sin[s] * cos - turn_cos[s] * sin
                if s == 0:
                    cos, sin = jnp.where(second, 0.0, cos), jnp.where(second, 0.0, sin)
                else:
                    cos, sin = jnp.where(second, cos, 0.0), jnp.where(second, sin, 0.0)
                waves[rows, at : at + FB] = cos.astype(BF16)
                waves[rows, at + FB : at + 2 * FB] = sin.astype(BF16)
            return carry

        each(own, own_waves)


def weigh_kernel(
    position_ref,
    near_ref,
    far_ref,
    own_cols,
    projection_ref,
    *rest,
):
    *numbers, ghost_cols, weight, weight_turned, waves, rows_in = rest
    own = position_ref.shape[2]
    sent = near_ref.shape[1]
    features = projection_ref.shape[2]

    rows_in[...] = jnp.zeros_like(rows_in)
    rows_in[0:4, 0:sent] = near_ref[...]
    rows_in[0:4, sent : 2 * sent] = far_ref[...]
    ghost_cols[...] = rows_in[...].T
    here = [position_ref[a] for a in range(3)]

    for k, number_ref in enumerate(numbers):
        first = k * number_ref.shape[0]
        cols, skip = (own_cols, first) if first < own else (ghost_cols, first - own)

        def weigh(c, carry):
            there = cols[chunk_rows(c, skip), :]
            square = 0.0
            for a in range(3):
                d = there[:, a : a + 1] - here[a]
                square = square + d * d
            weight[chunk_rows(c, first), :] = number_ref[chunk_rows(c), :] * jnp.exp(
                square * (-1.0 / (2.0 * WIDTH * WIDTH))
            )
            return carry

        each(number_ref.shape[0], weigh)
    weight_turned[...] = weight[...].T.astype(BF16)

    for block in range(features // FB):
        mine = slice(block * FB, (block + 1) * FB)
        base = block * 4 * FB
        wave = [
            [projection_ref[a, s : s + 1, mine] * TURN for a in range(3)] for s in range(2)
        ]

        def ghost_waves(c, carry):
            rows = chunk_rows(c)
            there = ghost_cols[rows, :]
            x, y, z = (jnp.broadcast_to(there[:, a : a + 1], (ROWS, FB)) for a in range(3))
            second = jnp.broadcast_to(there[:, 3:4], (ROWS, FB)) > 0.5
            px, py, pz = (jnp.where(second, wave[1][a], wave[0][a]) for a in range(3))
            cos, sin = cos_sin(x * px + y * py + z * pz)
            for s in range(2):
                at = base + s * 2 * FB
                for k, part in enumerate((cos, sin)):
                    if s == 0:
                        part = jnp.where(second, 0.0, part)
                    else:
                        part = jnp.where(second, part, 0.0)
                    waves[rows, at + k * FB : at + (k + 1) * FB] = part.astype(BF16)
            return carry

        each(2 * sent, ghost_waves)


def describe_kernel(
    weight_turned,
    own_waves,
    ghost_waves,
    turned,
    sines,
    low,
    sums,
):
    own = weight_turned.shape[0]
    features = low.shape[1]
    for block in range(features // FB):
        these = slice(block * 4 * FB, (block + 1) * 4 * FB)
        sums[:, these] = jnp.dot(
            weight_turned[:, 0:own], own_waves[:, these], preferred_element_type=F32
        ) + jnp.dot(weight_turned[:, own:], ghost_waves[:, these], preferred_element_type=F32)

    for block in range(features // FB):
        mine = slice(block * FB, (block + 1) * FB)
        base = block * 4 * FB

        def describe(c, carry):
            rows = chunk_rows(c)
            total = 0.0
            for s in range(2):
                at = base + s * 2 * FB
                tr, ti = turned[rows, at : at + FB], turned[rows, at + FB : at + 2 * FB]
                ur, ui = sums[rows, at : at + FB], sums[rows, at + FB : at + 2 * FB]
                total = total + (tr * ur - ti * ui)
                first = s * features + block * FB
                sines[rows, first : first + FB] = tr * ui + ti * ur
            low[rows, mine] = total.astype(BF16)
            return carry

        each(own, describe)


def fold(value):
    total = value[:, 0:LANES]
    for k in range(1, value.shape[1] // LANES):
        total = total + value[:, k * LANES : (k + 1) * LANES]
    return total


def pull_rows(
    along_first, first, cols, waves, weight, spread, projection_ref, here, parts, back, product
):
    count = cols.shape[0]
    features = projection_ref.shape[2]
    held = weight[first : first + count, :].astype(BF16)

    def back_of(block):
        these = slice(block * 4 * FB, (block + 1) * 4 * FB)
        back[:, these] = jnp.dot(held, spread[:, these], preferred_element_type=F32)

    def pull_block(block):
        mine = slice(block * FB, (block + 1) * FB)
        base = block * 4 * FB
        raw = [[projection_ref[a, s : s + 1, mine] for a in range(3)] for s in range(2)]

        def pull(c, carry):
            rows = chunk_rows(c)
            second = jnp.broadcast_to(cols[rows, 3:4], (ROWS, FB)) > 0.5
            total = 0.0
            for s in range(2):
                at = base + s * 2 * FB
                er = waves[rows, at : at + FB].astype(F32)
                ei = waves[rows, at + FB : at + 2 * FB].astype(F32)
                vr = back[rows, at : at + FB]
                vi = back[rows, at + FB : at + 2 * FB]
                total = total + (ei * vr - er * vi)
            for a in range(3):
                coeff = jnp.where(second, raw[1][a], raw[0][a])
                parts[a, rows, :] = parts[a, rows, :] + fold(total * coeff)
            return carry

        each(count, pull)

    def along(c, carry):
        rows = chunk_rows(c)
        there = cols[rows, :]
        z = weight[chunk_rows(c, first), :] * product[rows, :] * (1.0 / (WIDTH * WIDTH))
        out = []
        for a in range(3):
            pull_a = z * (there[:, a : a + 1] - here[a])
            parts[a, rows, :] = parts[a, rows, :] + fold(pull_a)
            total = pull_a[0:8]
            for k in range(1, ROWS // 8):
                total = total + pull_a[8 * k : 8 * k + 8]
            out.append(carry[a] + total)
        return tuple(out)

    def product_of():
        product[...] = lax.dot_general(
            waves[...], spread[...], (((1,), (1,)), ((), ())), preferred_element_type=F32
        )

    start = tuple(jnp.zeros((8, here[0].shape[1]), F32) for _ in range(3))
    blocks = range(features // FB)
    if along_first:
        product_of()
        for block in blocks:
            back_of(block)
        centre = each(count, along, carry=start)
        for block in blocks:
            pull_block(block)
    else:
        for block in blocks:
            back_of(block)
            pull_block(block)
        product_of()
        centre = each(count, along, carry=start)
    return centre


def ghost_force_kernel(
    low,
    half_ref,
    other_ref,
    own_cols,
    turned,
    weight,
    waves,
    cols,
    position_ref,
    projection_ref,
    grad,
    spread,
    centre_ref,
    near_ref,
    far_ref,
    back,
    product,
    parts,
):
    own, features = grad.shape
    sent = near_ref.shape[1]
    here = [position_ref[a] for a in range(3)]
    mine_is = core_of().astype(F32)
    grad[...] = jnp.where(
        own_cols[:, 3:4] == mine_is,
        jnp.dot(low[...], half_ref[...], preferred_element_type=F32),
        jnp.dot(low[...], other_ref[...], preferred_element_type=F32),
    )
    for block in range(features // FB):
        mine = slice(block * FB, (block + 1) * FB)
        base = block * 4 * FB

        def spread_out(c, carry):
            rows = chunk_rows(c)
            g = grad[rows, mine]
            for s in range(2):
                at = base + s * 2 * FB
                spread[rows, at : at + FB] = (g * turned[rows, at : at + FB]).astype(BF16)
                spread[rows, at + FB : at + 2 * FB] = (
                    -g * turned[rows, at + FB : at + 2 * FB]
                ).astype(BF16)
            return carry

        each(own, spread_out)

    parts[...] = jnp.zeros_like(parts)
    centre = pull_rows(
        True, own, cols, waves, weight, spread, projection_ref, here, parts, back, product
    )
    for a in range(3):
        row = jnp.sum(parts[a].T, axis=0, keepdims=True)
        centre_ref[a : a + 1, :] = jnp.sum(centre[a], axis=0, keepdims=True)
        near_ref[a : a + 1, :] = row[:, 0:sent]
        far_ref[a : a + 1, :] = row[:, sent:]


def own_force_kernel(
    grad,
    spread,
    sines,
    waves,
    weight,
    cols,
    position_ref,
    centre_ref,
    projection_ref,
    force_ref,
    back,
    product,
    parts,
):
    own, features = grad.shape
    here = [position_ref[a] for a in range(3)]
    raw = [[projection_ref[a, s : s + 1, :] for a in range(3)] for s in range(2)]

    def turn(c, carry):
        rows = chunk_rows(c)
        g = grad[rows, :]
        t0 = g * sines[rows, 0:features]
        t1 = g * sines[rows, features : 2 * features]
        for a in range(3):
            parts[a, rows, :] = -fold(t0 * raw[0][a] + t1 * raw[1][a])
        return carry

    each(own, turn)
    centre = pull_rows(
        False, 0, cols, waves, weight, spread, projection_ref, here, parts, back, product
    )
    for a in range(3):
        row = jnp.sum(parts[a].T, axis=0, keepdims=True)
        force_ref[a : a + 1, :] = (
            row - jnp.sum(centre[a], axis=0, keepdims=True) - centre_ref[a : a + 1, :]
        )


def routed(block, axis, source):
    return lax.ppermute(block, axis, [(source(i), i) for i in range(lax.axis_size(axis))])


def near_pair(block):
    return routed(block, "dom", lambda i: i ^ 1)


def far_pair(block):
    return routed(block, "dom", lambda i: (i - 1 + i % 2 * 2) % lax.axis_size("dom"))


def across(block):
    beads = lax.axis_size("bead")
    route = [(i ^ (2 * beads + 4), i) for i in range(beads * lax.axis_size("dom"))]
    return lax.ppermute(block, ("dom", "bead"), route)


def even_bead(block):
    return routed(block, "bead", lambda i: i ^ 1)


def odd_bead(block):
    return routed(block, "bead", lambda i: (i - 1 + i % 2 * 2) % lax.axis_size("bead"))


def after(value, *others):
    return lax.optimization_barrier((value, others))[0]


def matrix_part(points, point_weights):
    dom = lax.axis_index("dom")
    which, height = dom % 2, points.shape[2] // 4
    p = lax.dynamic_index_in_dim(points, which, 0, keepdims=False).astype(F32)
    w = lax.dynamic_index_in_dim(point_weights, which, 0, keepdims=False).astype(F32)
    left = lax.dynamic_slice_in_dim(p, dom // 4 * height, height, axis=1)
    return lax.dot_general(
        left * (2.0 * w)[:, None],
        p,
        (((0,), (0,)), ((), ())),
        precision=lax.Precision.HIGHEST,
        preferred_element_type=F32,
    )


def packed_places(atoms):
    pieces = atoms // LANES
    for axis_id in range(3):
        for part in range(3):
            for piece in range(pieces):
                k = (axis_id * 3 + part) * pieces + piece
                yield axis_id, part, piece, k // 3, k % 3


def add_pack_kernel(part_ref, other_ref, position_ref, total_ref, sent_ref, *rest):
    rows = part_ref.shape[0]
    total = part_ref[...] + other_ref[0:rows, :].astype(F32)
    total_ref[...] = total
    sent_ref[0:rows, :] = total.astype(BF16)
    if len(rest) > 1:
        unpack(other_ref, rows, rest[0])
    packed = rest[-1]
    packed[...] = jnp.zeros_like(packed)
    split = []
    for a in range(3):
        left = position_ref[a]
        split.append([])
        for _ in range(3):
            part = left.astype(BF16).astype(F32)
            split[a].append(part)
            left = left - part
    for a, part, piece, row, column in packed_places(position_ref.shape[2]):
        packed[row : row + 1, column * LANES : (column + 1) * LANES] = split[a][part][
            :, piece * LANES : (piece + 1) * LANES
        ]
    sent_ref[rows : rows + PACKED, :] = packed[...].astype(BF16)


def unpack(sent_ref, rows, position_ref):
    packed = sent_ref[rows : rows + PACKED, :].astype(F32)
    sums = {}
    for a, part, piece, row, column in packed_places(position_ref.shape[2]):
        value = packed[row : row + 1, column * LANES : (column + 1) * LANES]
        sums[a, piece] = value if part == 0 else sums[a, piece] + value
    for (a, piece), value in sums.items():
        position_ref[a, :, piece * LANES : (piece + 1) * LANES] = value


def add_unpack_kernel(part_ref, other_ref, held_ref, position_ref):
    rows = part_ref.shape[0]
    held_ref[...] = (part_ref[...] + other_ref[0:rows, :].astype(F32)).astype(BF16)
    unpack(other_ref, rows, position_ref)


def block_at(k):
    width = 128
    return pl.ds(pl.multiple_of(k % 4 * width, width), width)


def cut_kernel(part_ref, *outs):
    height = lax.axis_index("dom") // 4
    for j in range(3):
        block = part_ref[:, block_at(height + j)]
        for out in outs:
            out[:, j * LANES : (j + 1) * LANES] = block.astype(out.dtype)


def ring_kernel(*refs):
    *pieces, out_ref = refs
    height = lax.axis_index("dom") // 4
    for k, piece in enumerate(pieces):
        row = height + 4 - k
        for j in range(3):
            out_ref[block_at(row), block_at(row + j)] = piece[:, j * LANES : (j + 1) * LANES]
        turned = piece[:, LANES : 2 * LANES].astype(F32).T.astype(BF16)
        out_ref[block_at(row + 1), block_at(row)] = turned


def shards(
    positions,
    velocities,
    species,
    neighbours,
    neighbour_count,
    send_lists,
    projection,
    phase_shift,
    points,
    point_weights,
):
    own, sent = positions.shape[2], send_lists.shape[1]
    ghosts = 2 * sent
    everyone = own + ghosts
    features = points.shape[2]
    shape = jax.ShapeDtypeStruct
    species = species.reshape(1, own)
    position, velocity = positions.transpose(1, 0, 2), velocities.transpose(1, 0, 2)
    projection = projection.transpose(1, 0, 2)
    sends = (shape((4, sent), F32),) * 2
    wide = pltpu.VMEM((LANES, own), F32)
    slab = (features // 4, features // 4 * 3)
    counts = neighbour_count.reshape(1, own)

    def count(part, neighbours):
        return call(
            functools.partial(count_kernel, part),
            shape((ghosts, own), F32),
            [pltpu.VMEM((NEIGH, own), F32)],
        )(neighbours, counts)

    own_call = call(
        own_kernel,
        (
            shape((own, LANES), F32),
            shape((own, 4 * features), BF16),
            shape((own, 4 * features), F32),
        ),
        [wide],
        LIMIT,
    )
    weigh_call = call(
        weigh_kernel,
        (
            shape((ghosts, LANES), F32),
            shape((everyone, own), F32),
            shape((own, everyone), BF16),
            shape((ghosts, 4 * features), BF16),
        ),
        [pltpu.VMEM((LANES, ghosts), F32)],
        LIMIT,
    )
    describe_call = call(
        describe_kernel,
        (shape((own, 2 * features), F32), shape((own, features), BF16)),
        [pltpu.VMEM((own, 4 * features), F32)],
        LIMIT,
    )
    ghost_force_call = call(
        ghost_force_kernel,
        (
            shape((own, features), F32),
            shape((own, 4 * features), BF16),
            shape((3, own), F32),
            shape((3, sent), F32),
            shape((3, sent), F32),
        ),
        [
            pltpu.VMEM((ghosts, 4 * features), F32),
            pltpu.VMEM((ghosts, own), F32),
            pltpu.VMEM((3, ghosts, LANES), F32),
        ],
        LIMIT,
    )
    own_force_call = call(
        own_force_kernel,
        shape((3, own), F32),
        [
            pltpu.VMEM((own, 4 * features), F32),
            pltpu.VMEM((own, own), F32),
            pltpu.VMEM((3, own, LANES), F32),
        ],
        LIMIT,
    )

    to_near, to_far = call(first_kernel, sends, [wide])(position, species, send_lists)
    part, sent_part = call(cut_kernel, (shape(slab, F32), shape(slab, BF16)))(
        matrix_part(points, point_weights)
    )
    for step in range(STEPS):
        last = step == STEPS - 1
        if step == 0:
            other = across(sent_part)
            to_far, to_near = after(to_far, sent_part), after(to_near, sent_part)
        from_far = far_pair(to_far)
        from_near = near_pair(to_near)
        if step == 0:
            number = [count(k, neighbours) for k in range(2)]
            with_positions = shape((slab[0] + PACKED, slab[1]), BF16)
            packed = [pltpu.VMEM((PACKED, slab[1]), F32)]
            part, held = call(add_pack_kernel, (shape(slab, F32), with_positions), packed)(
                part, after(other, from_far, from_near, *number), position
            )
            other = even_bead(held)
        start = after(position, held) if step == 0 else position
        cols, waves, turned = own_call(start, species, projection, phase_shift)
        if step == 0:
            bead_shape = shape(position.shape, F32)
            part, held, one_bead = call(
                add_pack_kernel, (shape(slab, F32), with_positions, bead_shape), packed
            )(part, after(other, cols), position)
            other = odd_bead(held)
            number.append(count(2, after(neighbours, held)))
            state = weigh_call(
                after(position, held), from_near, from_far, cols, projection, *number
            )
            ghost_cols, weight, weight_turned, ghost_waves = state
            held, other_bead = call(add_unpack_kernel, (shape(slab, BF16), bead_shape))(
                part, after(other, *state)
            )
            pieces = [held] + [routed(held, "dom", lambda i: (i - 4 * k) % 16) for k in (1, 2, 3)]
            sines, low = describe_call(after(weight_turned, held), waves, ghost_waves, turned)
            half = call(ring_kernel, shape((features, features), BF16))(
                pieces[0], *[after(piece, low) for piece in pieces[1:]]
            )
            other_half = near_pair(half)
        else:
            one_bead = even_bead(after(position, cols, from_far, from_near))
            ghost_cols, weight, weight_turned, ghost_waves = weigh_call(
                position, from_near, from_far, cols, projection, *number
            )
            sines, low = describe_call(weight_turned, waves, ghost_waves, turned)
            other_bead = odd_bead(after(position, low))
        grad, spread, centre, near_force, far_force = ghost_force_call(
            low,
            half,
            other_half,
            cols,
            turned,
            weight,
            ghost_waves,
            ghost_cols,
            position,
            projection,
        )
        far_back = far_pair(far_force)
        near_back = near_pair(near_force)
        force = own_force_call(
            grad, spread, sines, waves, weight, cols, position, centre, projection
        )
        moved = shape(position.shape, F32)
        position, velocity, *rest = call(
            functools.partial(update_kernel, last),
            (moved, moved) + (() if last else sends),
            [pltpu.VMEM((LANES, sent), F32), wide],
        )(
            force,
            near_back,
            far_back,
            send_lists,
            position,
            velocity,
            other_bead,
            one_bead,
            species,
        )
        if not last:
            to_near, to_far = rest
    return (position.transpose(1, 0, 2), velocity.transpose(1, 0, 2))


def solution(mesh):
    placed = (
        P("bead", None, "dom"),
        P("bead", None, "dom"),
        P("dom"),
        P(None, "dom"),
        P("dom"),
        P(None, "dom"),
        P(),
        P(),
        P(None, "bead", None),
        P(None, "bead"),
    )
    return jax.shard_map(
        shards,
        mesh=mesh,
        in_specs=placed,
        out_specs=(P("bead", None, "dom"), P("bead", None, "dom")),
        check_vma=False,
    )
```

```python
import functools

import jax
import jax.numpy as jnp
from jax import lax
from jax.experimental import pallas as pl
from jax.experimental.pallas import tpu as pltpu
from jax.sharding import PartitionSpec as P

NEIGH = 32
STEPS = 2

WIDTH = 1.5
DT = 0.1
KAPPA = 0.5

F32, BF16 = jnp.float32, jnp.bfloat16
LANES = 128
ROWS = 32
FB = 256
TURN = 0.15915494309189535
SIN = (3.1415927410125732, -5.167710304260254, 2.550077438354492, -0.5982903838157654, 0.07765591144561768)
COS = (0.9999999403953552, -4.934792995452881, 4.05841064453125, -1.3318729400634766, 0.21968242526054382)
VMEM = pl.BlockSpec(memory_space=pltpu.VMEM)
MIB = 1024 * 1024
LIMIT = 16


def call(body, outs, scratch=(), limit=8):
    return pl.pallas_call(
        body,
        out_shape=outs,
        out_specs=jax.tree.map(lambda _: VMEM, outs),
        scratch_shapes=scratch,
        compiler_params=pltpu.CompilerParams(vmem_limit_bytes=limit * MIB),
    )


def cos_sin(turns):
    f = turns - jnp.round(turns)
    g = f * f
    s, c = SIN[-1], COS[-1]
    for low in SIN[-2::-1]:
        s = s * g + low
    for low in COS[-2::-1]:
        c = c * g + low
    s = s * f
    twice = s + s
    return 1.0 - twice * s, twice * c


def core_of():
    return lax.axis_index("dom") % 2


def count_kernel(part, neighbours_ref, count_ref, number_ref, named):
    rows, atoms = number_ref.shape
    slot = lax.broadcasted_iota(jnp.int32, neighbours_ref.shape, 0)
    row = jnp.where(slot < count_ref[...], neighbours_ref[...] - part * rows, -1)
    if part * rows >= atoms:
        swapped = jnp.where(row >= rows // 2, row - rows // 2, row + rows // 2)
        row = jnp.where((core_of() == 0) & (row >= 0), swapped, row)
    named[...] = jnp.where((row >= 0) & (row < rows), row, -1).astype(F32)
    one, zero = jnp.ones((), BF16), jnp.zeros((), BF16)
    step = 2 * ROWS
    for start in range(0, rows, step):
        local = (lax.broadcasted_iota(jnp.int32, (step, atoms), 0) + start).astype(F32).astype(BF16)
        total = jnp.zeros((step, atoms), BF16)
        for k in range(NEIGH):
            total = total + jnp.where(local == named[k : k + 1, :].astype(BF16), one, zero)
        number_ref[start : start + step, :] = total.astype(F32)


def near_far_lists(lists_ref):
    core = core_of()
    return [lists_ref[pl.ds(1 - core, 1), :], lists_ref[pl.ds(core, 1), :]]


def gather_rows(columns, list_row, count):
    atoms, listed = columns.shape[0], list_row.shape[1]
    hit = lax.broadcasted_iota(jnp.int32, (atoms, listed), 0) == list_row
    return [
        jnp.sum(jnp.where(hit, columns[:, a : a + 1], 0.0), axis=0, keepdims=True)
        for a in range(count)
    ]


def send_rows(position_rows, species_row, lists, near_ref, far_ref, wide):
    wide[...] = jnp.zeros_like(wide)
    for a in range(3):
        wide[a : a + 1, :] = position_rows[a]
    wide[3:4, :] = species_row
    columns = wide[...].T
    for out, listed in zip((near_ref, far_ref), lists):
        for a, row in enumerate(gather_rows(columns, listed, 4)):
            out[a : a + 1, :] = row


def first_kernel(position_ref, species_ref, lists_ref, near_ref, far_ref, wide):
    rows = [position_ref[a] for a in range(3)]
    lists = near_far_lists(lists_ref)
    send_rows(rows, species_ref[...].astype(F32), lists, near_ref, far_ref, wide)


def update_kernel(
    last,
    force_ref,
    near_back_ref,
    far_back_ref,
    lists_ref,
    position_ref,
    velocity_ref,
    one_bead_ref,
    other_bead_ref,
    species_ref,
    new_position_ref,
    new_velocity_ref,
    *rest,
):
    atoms = position_ref.shape[2]
    listed = lists_ref.shape[1]
    wide = rest[-1]
    back = rest[-2]
    lists = near_far_lists(lists_ref)
    extra = [0.0, 0.0, 0.0]
    for names, ref in zip(lists, (near_back_ref, far_back_ref)):
        back[...] = jnp.zeros_like(back)
        back[0:3, :] = ref[...]
        back[3:4, :] = names.astype(F32)
        values = back[...].T
        hit = lax.broadcasted_iota(jnp.int32, (listed, atoms), 1).astype(F32) == values[:, 3:4]
        for a in range(3):
            extra[a] = extra[a] + jnp.sum(
                jnp.where(hit, values[:, a : a + 1], 0.0), axis=0, keepdims=True
            )
    species = species_ref[...]
    mass = jnp.where(species == 0, 16.0, 1.0)
    rows = []
    for a in range(3):
        here = position_ref[a]
        chain = 2.0 * here - one_bead_ref[a] - other_bead_ref[a]
        total = force_ref[a : a + 1, :] + extra[a] - KAPPA * mass * chain
        velocity = velocity_ref[a] + DT * (total / mass)
        place = here + DT * velocity
        new_velocity_ref[a] = velocity
        new_position_ref[a] = place
        rows.append(place)
    if not last:
        send_rows(rows, species.astype(F32), lists, rest[0], rest[1], wide)


def each(count, body, carry=0):
    for c in range(count // ROWS):
        carry = body(c, carry)
    return carry


def chunk_rows(c, first=0):
    return slice(first + c * ROWS, first + (c + 1) * ROWS)


def own_kernel(
    position_ref,
    species_ref,
    projection_ref,
    shift_ref,
    cols,
    waves,
    turned,
    rows_in,
):
    own = position_ref.shape[2]
    features = projection_ref.shape[2]
    rows_in[...] = jnp.zeros_like(rows_in)
    for a in range(3):
        rows_in[a : a + 1, :] = position_ref[a]
    rows_in[3:4, :] = species_ref[...].astype(F32)
    cols[...] = rows_in[...].T

    shift_cos, shift_sin = cos_sin(shift_ref[...] * TURN)
    for block in range(features // FB):
        mine = slice(block * FB, (block + 1) * FB)
        base = block * 4 * FB
        wave = [
            [projection_ref[a, s : s + 1, mine] * TURN for a in range(3)] for s in range(2)
        ]
        turn_cos = [shift_cos[s : s + 1, mine] for s in range(2)]
        turn_sin = [shift_sin[s : s + 1, mine] for s in range(2)]

        def own_waves(c, carry):
            rows = chunk_rows(c)
            there = cols[rows, :]
            x, y, z = (jnp.broadcast_to(there[:, a : a + 1], (ROWS, FB)) for a in range(3))
            second = jnp.broadcast_to(there[:, 3:4], (ROWS, FB)) > 0.5
            for s in range(2):
                cos, sin = cos_sin(x * wave[s][0] + y * wave[s][1] + z * wave[s][2])
                at = base + s * 2 * FB
                turned[rows, at : at + FB] = turn_cos[s] * cos + turn_sin[s] * sin
                turned[rows, at + FB : at + 2 * FB] = turn_sin[s] * cos - turn_cos[s] * sin
                if s == 0:
                    cos, sin = jnp.where(second, 0.0, cos), jnp.where(second, 0.0, sin)
                else:
                    cos, sin = jnp.where(second, cos, 0.0), jnp.where(second, sin, 0.0)
                waves[rows, at : at + FB] = cos.astype(BF16)
                waves[rows, at + FB : at + 2 * FB] = sin.astype(BF16)
            return carry

        each(own, own_waves)


def weigh_kernel(
    position_ref,
    near_ref,
    far_ref,
    own_cols,
    projection_ref,
    *rest,
):
    *numbers, ghost_cols, weight, weight_turned, waves, rows_in = rest
    own = position_ref.shape[2]
    sent = near_ref.shape[1]
    features = projection_ref.shape[2]

    rows_in[...] = jnp.zeros_like(rows_in)
    rows_in[0:4, 0:sent] = near_ref[...]
    rows_in[0:4, sent : 2 * sent] = far_ref[...]
    ghost_cols[...] = rows_in[...].T
    here = [position_ref[a] for a in range(3)]

    for k, number_ref in enumerate(numbers):
        first = k * number_ref.shape[0]
        cols, skip = (own_cols, first) if first < own else (ghost_cols, first - own)

        def weigh(c, carry):
            there = cols[chunk_rows(c, skip), :]
            square = 0.0
            for a in range(3):
                d = there[:, a : a + 1] - here[a]
                square = square + d * d
            weight[chunk_rows(c, first), :] = number_ref[chunk_rows(c), :] * jnp.exp(
                square * (-1.0 / (2.0 * WIDTH * WIDTH))
            )
            return carry

        each(number_ref.shape[0], weigh)
    weight_turned[...] = weight[...].T.astype(BF16)

    for block in range(features // FB):
        mine = slice(block * FB, (block + 1) * FB)
        base = block * 4 * FB
        wave = [
            [projection_ref[a, s : s + 1, mine] * TURN for a in range(3)] for s in range(2)
        ]

        def ghost_waves(c, carry):
            rows = chunk_rows(c)
            there = ghost_cols[rows, :]
            x, y, z = (jnp.broadcast_to(there[:, a : a + 1], (ROWS, FB)) for a in range(3))
            second = jnp.broadcast_to(there[:, 3:4], (ROWS, FB)) > 0.5
            px, py, pz = (jnp.where(second, wave[1][a], wave[0][a]) for a in range(3))
            cos, sin = cos_sin(x * px + y * py + z * pz)
            for s in range(2):
                at = base + s * 2 * FB
                for k, part in enumerate((cos, sin)):
                    if s == 0:
                        part = jnp.where(second, 0.0, part)
                    else:
                        part = jnp.where(second, part, 0.0)
                    waves[rows, at + k * FB : at + (k + 1) * FB] = part.astype(BF16)
            return carry

        each(2 * sent, ghost_waves)


def describe_kernel(
    weight_turned,
    own_waves,
    ghost_waves,
    turned,
    sines,
    low,
    sums,
):
    own = weight_turned.shape[0]
    features = low.shape[1]
    for block in range(features // FB):
        mine = slice(block * FB, (block + 1) * FB)
        base = block * 4 * FB
        sums[...] = jnp.dot(
            weight_turned[:, 0:own], own_waves[:, base : base + 4 * FB], preferred_element_type=F32
        ) + jnp.dot(
            weight_turned[:, own:], ghost_waves[:, base : base + 4 * FB], preferred_element_type=F32
        )

        def describe(c, carry):
            rows = chunk_rows(c)
            total = 0.0
            for s in range(2):
                at = base + s * 2 * FB
                tr, ti = turned[rows, at : at + FB], turned[rows, at + FB : at + 2 * FB]
                ur = sums[rows, s * 2 * FB : s * 2 * FB + FB]
                ui = sums[rows, s * 2 * FB + FB : s * 2 * FB + 2 * FB]
                total = total + (tr * ur - ti * ui)
                first = s * features + block * FB
                sines[rows, first : first + FB] = tr * ui + ti * ur
            low[rows, mine] = total.astype(BF16)
            return carry

        each(own, describe)


def weigh_describe_kernel(
    position_ref, near_ref, far_ref, own_cols, projection_ref, own_waves, turned, *rest
):
    *numbers, ghost_cols, weight, ghost_waves, sines, low, rows_in, weight_turned, sums = rest
    weigh_kernel(
        position_ref,
        near_ref,
        far_ref,
        own_cols,
        projection_ref,
        *numbers,
        ghost_cols,
        weight,
        weight_turned,
        ghost_waves,
        rows_in,
    )
    describe_kernel(weight_turned, own_waves, ghost_waves, turned, sines, low, sums)


def fold(value):
    total = value[:, 0:LANES]
    for k in range(1, value.shape[1] // LANES):
        total = total + value[:, k * LANES : (k + 1) * LANES]
    return total


def pull_rows(first, cols, waves, weight, spread, projection_ref, here, parts, back, product):
    count = cols.shape[0]
    features = projection_ref.shape[2]
    held = weight[first : first + count, :].astype(BF16)
    for block in range(features // FB):
        mine = slice(block * FB, (block + 1) * FB)
        base = block * 4 * FB
        raw = [[projection_ref[a, s : s + 1, mine] for a in range(3)] for s in range(2)]
        back[...] = jnp.dot(held, spread[:, base : base + 4 * FB], preferred_element_type=F32)

        def pull(c, carry):
            rows = chunk_rows(c)
            second = jnp.broadcast_to(cols[rows, 3:4], (ROWS, FB)) > 0.5
            total = 0.0
            for s in range(2):
                at = base + s * 2 * FB
                er = waves[rows, at : at + FB].astype(F32)
                ei = waves[rows, at + FB : at + 2 * FB].astype(F32)
                vr = back[rows, s * 2 * FB : s * 2 * FB + FB]
                vi = back[rows, s * 2 * FB + FB : s * 2 * FB + 2 * FB]
                total = total + (ei * vr - er * vi)
            for a in range(3):
                coeff = jnp.where(second, raw[1][a], raw[0][a])
                parts[a, rows, :] = parts[a, rows, :] + fold(total * coeff)
            return carry

        each(count, pull)

    product[...] = lax.dot_general(
        waves[...], spread[...], (((1,), (1,)), ((), ())), preferred_element_type=F32
    )

    def along(c, carry):
        rows = chunk_rows(c)
        there = cols[rows, :]
        z = weight[chunk_rows(c, first), :] * product[rows, :] * (1.0 / (WIDTH * WIDTH))
        out = []
        for a in range(3):
            pull_a = z * (there[:, a : a + 1] - here[a])
            parts[a, rows, :] = parts[a, rows, :] + fold(pull_a)
            total = pull_a[0:8]
            for k in range(1, ROWS // 8):
                total = total + pull_a[8 * k : 8 * k + 8]
            out.append(carry[a] + total)
        return tuple(out)

    start = tuple(jnp.zeros((8, here[0].shape[1]), F32) for _ in range(3))
    return each(count, along, carry=start)


def ghost_force_kernel(
    low,
    half_ref,
    other_ref,
    own_cols,
    turned,
    weight,
    waves,
    cols,
    position_ref,
    projection_ref,
    grad,
    spread,
    centre_ref,
    near_ref,
    far_ref,
    back,
    product,
    parts,
):
    own, features = grad.shape
    sent = near_ref.shape[1]
    here = [position_ref[a] for a in range(3)]
    mine_is = core_of().astype(F32)
    grad[...] = jnp.where(
        own_cols[:, 3:4] == mine_is,
        jnp.dot(low[...], half_ref[...], preferred_element_type=F32),
        jnp.dot(low[...], other_ref[...], preferred_element_type=F32),
    )
    for block in range(features // FB):
        mine = slice(block * FB, (block + 1) * FB)
        base = block * 4 * FB

        def spread_out(c, carry):
            rows = chunk_rows(c)
            g = grad[rows, mine]
            for s in range(2):
                at = base + s * 2 * FB
                spread[rows, at : at + FB] = (g * turned[rows, at : at + FB]).astype(BF16)
                spread[rows, at + FB : at + 2 * FB] = (
                    -g * turned[rows, at + FB : at + 2 * FB]
                ).astype(BF16)
            return carry

        each(own, spread_out)

    parts[...] = jnp.zeros_like(parts)
    centre = pull_rows(
        own, cols, waves, weight, spread, projection_ref, here, parts, back, product
    )
    for a in range(3):
        row = jnp.sum(parts[a].T, axis=0, keepdims=True)
        centre_ref[a : a + 1, :] = jnp.sum(centre[a], axis=0, keepdims=True)
        near_ref[a : a + 1, :] = row[:, 0:sent]
        far_ref[a : a + 1, :] = row[:, sent:]


def own_force_kernel(
    grad,
    spread,
    sines,
    waves,
    weight,
    cols,
    position_ref,
    centre_ref,
    projection_ref,
    force_ref,
    back,
    product,
    parts,
):
    own, features = grad.shape
    here = [position_ref[a] for a in range(3)]
    raw = [[projection_ref[a, s : s + 1, :] for a in range(3)] for s in range(2)]

    def turn(c, carry):
        rows = chunk_rows(c)
        g = grad[rows, :]
        t0 = g * sines[rows, 0:features]
        t1 = g * sines[rows, features : 2 * features]
        for a in range(3):
            parts[a, rows, :] = -fold(t0 * raw[0][a] + t1 * raw[1][a])
        return carry

    each(own, turn)
    centre = pull_rows(
        0, cols, waves, weight, spread, projection_ref, here, parts, back, product
    )
    for a in range(3):
        row = jnp.sum(parts[a].T, axis=0, keepdims=True)
        force_ref[a : a + 1, :] = (
            row - jnp.sum(centre[a], axis=0, keepdims=True) - centre_ref[a : a + 1, :]
        )


def routed(block, axis, source):
    return lax.ppermute(block, axis, [(source(i), i) for i in range(lax.axis_size(axis))])


def near_pair(block):
    return routed(block, "dom", lambda i: i ^ 1)


def far_pair(block):
    return routed(block, "dom", lambda i: (i - 1 + i % 2 * 2) % lax.axis_size("dom"))


def across(block):
    beads = lax.axis_size("bead")
    route = [(i ^ (2 * beads + 4), i) for i in range(beads * lax.axis_size("dom"))]
    return lax.ppermute(block, ("dom", "bead"), route)


def even_bead(block):
    return routed(block, "bead", lambda i: i ^ 1)


def odd_bead(block):
    return routed(block, "bead", lambda i: (i - 1 + i % 2 * 2) % lax.axis_size("bead"))


def after(value, *others):
    return lax.optimization_barrier((value, others))[0]


def matrix_part(points, point_weights):
    dom = lax.axis_index("dom")
    which, height = dom % 2, points.shape[2] // 4
    p = lax.dynamic_index_in_dim(points, which, 0, keepdims=False).astype(F32)
    w = lax.dynamic_index_in_dim(point_weights, which, 0, keepdims=False).astype(F32)
    left = lax.dynamic_slice_in_dim(p, dom // 4 * height, height, axis=1)
    return lax.dot_general(
        left * (2.0 * w)[:, None],
        p,
        (((0,), (0,)), ((), ())),
        precision=lax.Precision.HIGHEST,
        preferred_element_type=F32,
    )


def add_kernel(part_ref, other_ref, *outs):
    total = part_ref[...] + other_ref[...].astype(F32)
    for out in outs:
        out[...] = total.astype(out.dtype)


def block_at(k):
    width = 128
    return pl.ds(pl.multiple_of(k % 4 * width, width), width)


def cut_kernel(part_ref, *outs):
    height = lax.axis_index("dom") // 4
    for j in range(3):
        block = part_ref[:, block_at(height + j)]
        for out in outs:
            out[:, j * LANES : (j + 1) * LANES] = block.astype(out.dtype)


def ring_kernel(*refs):
    *pieces, out_ref = refs
    height = lax.axis_index("dom") // 4
    for k, piece in enumerate(pieces):
        row = height + 4 - k
        for j in range(3):
            out_ref[block_at(row), block_at(row + j)] = piece[:, j * LANES : (j + 1) * LANES]
        turned = piece[:, LANES : 2 * LANES].astype(F32).T.astype(BF16)
        out_ref[block_at(row + 1), block_at(row)] = turned


def shards(
    positions,
    velocities,
    species,
    neighbours,
    neighbour_count,
    send_lists,
    projection,
    phase_shift,
    points,
    point_weights,
):
    own, sent = positions.shape[2], send_lists.shape[1]
    ghosts = 2 * sent
    everyone = own + ghosts
    features = points.shape[2]
    shape = jax.ShapeDtypeStruct
    species = species.reshape(1, own)
    position, velocity = positions.transpose(1, 0, 2), velocities.transpose(1, 0, 2)
    projection = projection.transpose(1, 0, 2)
    sends = (shape((4, sent), F32),) * 2
    wide = pltpu.VMEM((LANES, own), F32)
    slab = (features // 4, features // 4 * 3)
    counts = neighbour_count.reshape(1, own)

    def count(part, neighbours):
        return call(
            functools.partial(count_kernel, part),
            shape((ghosts, own), F32),
            [pltpu.VMEM((NEIGH, own), F32)],
        )(neighbours, counts)

    own_call = call(
        own_kernel,
        (
            shape((own, LANES), F32),
            shape((own, 4 * features), BF16),
            shape((own, 4 * features), F32),
        ),
        [wide],
        LIMIT,
    )
    weigh_call = call(
        weigh_kernel,
        (
            shape((ghosts, LANES), F32),
            shape((everyone, own), F32),
            shape((own, everyone), BF16),
            shape((ghosts, 4 * features), BF16),
        ),
        [pltpu.VMEM((LANES, ghosts), F32)],
        LIMIT,
    )
    describe_call = call(
        describe_kernel,
        (shape((own, 2 * features), F32), shape((own, features), BF16)),
        [pltpu.VMEM((own, 4 * FB), F32)],
        LIMIT,
    )
    weigh_describe_call = call(
        weigh_describe_kernel,
        (
            shape((ghosts, LANES), F32),
            shape((everyone, own), F32),
            shape((ghosts, 4 * features), BF16),
            shape((own, 2 * features), F32),
            shape((own, features), BF16),
        ),
        [
            pltpu.VMEM((LANES, ghosts), F32),
            pltpu.VMEM((own, everyone), BF16),
            pltpu.VMEM((own, 4 * FB), F32),
        ],
        LIMIT,
    )
    ghost_force_call = call(
        ghost_force_kernel,
        (
            shape((own, features), F32),
            shape((own, 4 * features), BF16),
            shape((3, own), F32),
            shape((3, sent), F32),
            shape((3, sent), F32),
        ),
        [
            pltpu.VMEM((ghosts, 4 * FB), F32),
            pltpu.VMEM((ghosts, own), F32),
            pltpu.VMEM((3, ghosts, LANES), F32),
        ],
        LIMIT,
    )
    own_force_call = call(
        own_force_kernel,
        shape((3, own), F32),
        [
            pltpu.VMEM((own, 4 * FB), F32),
            pltpu.VMEM((own, own), F32),
            pltpu.VMEM((3, own, LANES), F32),
        ],
        LIMIT,
    )

    to_near, to_far = call(first_kernel, sends, [wide])(position, species, send_lists)
    part, sent_part = call(cut_kernel, (shape(slab, F32), shape(slab, BF16)))(
        matrix_part(points, point_weights)
    )
    for step in range(STEPS):
        last = step == STEPS - 1
        if step == 0:
            other = across(sent_part)
            to_far, to_near = after(to_far, sent_part), after(to_near, sent_part)
        from_far = far_pair(to_far)
        from_near = near_pair(to_near)
        if step == 0:
            number = [count(k, neighbours) for k in range(2)]
            part, held = call(add_kernel, (shape(slab, F32), shape(slab, BF16)))(
                part, after(other, from_far, from_near, *number)
            )
            other = routed(held, "bead", lambda i: i ^ 1)
        start = after(position, held) if step == 0 else position
        cols, waves, turned = own_call(start, species, projection, phase_shift)
        if step == 0:
            part, held = call(add_kernel, (shape(slab, F32), shape(slab, BF16)))(
                part, after(other, cols)
            )
            other = routed(held, "bead", lambda i: i ^ 3)
            number.append(count(2, after(neighbours, held)))
            state = weigh_call(
                after(position, held), from_near, from_far, cols, projection, *number
            )
            ghost_cols, weight, weight_turned, ghost_waves = state
            held = call(add_kernel, (shape(slab, BF16),))(part, after(other, *state))[0]
            pieces = [held] + [routed(held, "dom", lambda i: (i - 4 * k) % 16) for k in (1, 2, 3)]
            one_bead = even_bead(after(position, held))
            sines, low = describe_call(after(weight_turned, held), waves, ghost_waves, turned)
            half = call(ring_kernel, shape((features, features), BF16))(
                pieces[0], *[after(piece, low, one_bead) for piece in pieces[1:]]
            )
            other_half = near_pair(half)
            other_bead = odd_bead(after(position, half))
        else:
            other_bead = odd_bead(after(position, cols, from_far, from_near))
            ghost_cols, weight, ghost_waves, sines, low = weigh_describe_call(
                position, from_near, from_far, cols, projection, waves, turned, *number
            )
            one_bead = even_bead(after(position, low, other_bead))
        grad, spread, centre, near_force, far_force = ghost_force_call(
            low,
            half,
            other_half,
            cols,
            turned,
            weight,
            ghost_waves,
            ghost_cols,
            position,
            projection,
        )
        far_back = far_pair(far_force)
        near_back = near_pair(near_force)
        force = own_force_call(
            grad, spread, sines, waves, weight, cols, position, centre, projection
        )
        moved = shape(position.shape, F32)
        position, velocity, *rest = call(
            functools.partial(update_kernel, last),
            (moved, moved) + (() if last else sends),
            [pltpu.VMEM((LANES, sent), F32), wide],
        )(
            force,
            near_back,
            far_back,
            send_lists,
            position,
            velocity,
            other_bead,
            one_bead,
            species,
        )
        if not last:
            to_near, to_far = rest
    return (position.transpose(1, 0, 2), velocity.transpose(1, 0, 2))


def solution(mesh):
    placed = (
        P("bead", None, "dom"),
        P("bead", None, "dom"),
        P("dom"),
        P(None, "dom"),
        P("dom"),
        P(None, "dom"),
        P(),
        P(),
        P(None, "bead", None),
        P(None, "bead"),
    )
    return jax.shard_map(
        shards,
        mesh=mesh,
        in_specs=placed,
        out_specs=(P("bead", None, "dom"), P("bead", None, "dom")),
        check_vma=False,
    )
```

```python
import functools

import jax
import jax.numpy as jnp
from jax import lax
from jax.experimental import pallas as pl
from jax.experimental.pallas import tpu as pltpu
from jax.sharding import PartitionSpec as P

NEIGH = 32
STEPS = 2

WIDTH = 1.5
DT = 0.1
KAPPA = 0.5

F32, BF16 = jnp.float32, jnp.bfloat16
LANES = 128
ROWS = 32
FB = 256
TURN = 0.15915494309189535
SIN = (3.1415927410125732, -5.167710304260254, 2.550077438354492, -0.5982903838157654, 0.07765591144561768)
COS = (0.9999999403953552, -4.934792995452881, 4.05841064453125, -1.3318729400634766, 0.21968242526054382)
VMEM = pl.BlockSpec(memory_space=pltpu.VMEM)
MIB = 1024 * 1024
LIMIT = 16


def call(body, outs, scratch=(), limit=8):
    return pl.pallas_call(
        body,
        out_shape=outs,
        out_specs=jax.tree.map(lambda _: VMEM, outs),
        scratch_shapes=scratch,
        compiler_params=pltpu.CompilerParams(vmem_limit_bytes=limit * MIB),
    )


def cos_sin(turns):
    f = turns - jnp.round(turns)
    g = f * f
    s, c = SIN[-1], COS[-1]
    for low in SIN[-2::-1]:
        s = s * g + low
    for low in COS[-2::-1]:
        c = c * g + low
    s = s * f
    twice = s + s
    return 1.0 - twice * s, twice * c


def core_of():
    return lax.axis_index("dom") % 2


def count_kernel(part, neighbours_ref, count_ref, number_ref, named):
    rows, atoms = number_ref.shape
    slot = lax.broadcasted_iota(jnp.int32, neighbours_ref.shape, 0)
    row = jnp.where(slot < count_ref[...], neighbours_ref[...] - part * rows, -1)
    if part * rows >= atoms:
        swapped = jnp.where(row >= rows // 2, row - rows // 2, row + rows // 2)
        row = jnp.where((core_of() == 0) & (row >= 0), swapped, row)
    named[...] = jnp.where((row >= 0) & (row < rows), row, -1).astype(F32)
    one, zero = jnp.ones((), BF16), jnp.zeros((), BF16)
    step = 2 * ROWS
    for start in range(0, rows, step):
        local = (lax.broadcasted_iota(jnp.int32, (step, atoms), 0) + start).astype(F32).astype(BF16)
        total = jnp.zeros((step, atoms), BF16)
        for k in range(NEIGH):
            total = total + jnp.where(local == named[k : k + 1, :].astype(BF16), one, zero)
        number_ref[start : start + step, :] = total.astype(F32)


def near_far_lists(lists_ref):
    core = core_of()
    return [lists_ref[pl.ds(1 - core, 1), :], lists_ref[pl.ds(core, 1), :]]


def gather_rows(columns, list_row, count):
    atoms, listed = columns.shape[0], list_row.shape[1]
    hit = lax.broadcasted_iota(jnp.int32, (atoms, listed), 0) == list_row
    return [
        jnp.sum(jnp.where(hit, columns[:, a : a + 1], 0.0), axis=0, keepdims=True)
        for a in range(count)
    ]


def send_rows(position_rows, species_row, lists, near_ref, far_ref, wide):
    wide[...] = jnp.zeros_like(wide)
    for a in range(3):
        wide[a : a + 1, :] = position_rows[a]
    wide[3:4, :] = species_row
    columns = wide[...].T
    for out, listed in zip((near_ref, far_ref), lists):
        for a, row in enumerate(gather_rows(columns, listed, 4)):
            out[a : a + 1, :] = row


def first_kernel(position_ref, species_ref, lists_ref, near_ref, far_ref, wide):
    rows = [position_ref[a] for a in range(3)]
    lists = near_far_lists(lists_ref)
    send_rows(rows, species_ref[...].astype(F32), lists, near_ref, far_ref, wide)


def update_kernel(
    last,
    force_ref,
    near_back_ref,
    far_back_ref,
    lists_ref,
    position_ref,
    velocity_ref,
    one_bead_ref,
    other_bead_ref,
    species_ref,
    new_position_ref,
    new_velocity_ref,
    *rest,
):
    atoms = position_ref.shape[2]
    listed = lists_ref.shape[1]
    wide = rest[-1]
    back = rest[-2]
    lists = near_far_lists(lists_ref)
    extra = [0.0, 0.0, 0.0]
    for names, ref in zip(lists, (near_back_ref, far_back_ref)):
        back[...] = jnp.zeros_like(back)
        back[0:3, :] = ref[...]
        back[3:4, :] = names.astype(F32)
        values = back[...].T
        hit = lax.broadcasted_iota(jnp.int32, (listed, atoms), 1).astype(F32) == values[:, 3:4]
        for a in range(3):
            extra[a] = extra[a] + jnp.sum(
                jnp.where(hit, values[:, a : a + 1], 0.0), axis=0, keepdims=True
            )
    species = species_ref[...]
    mass = jnp.where(species == 0, 16.0, 1.0)
    rows = []
    for a in range(3):
        here = position_ref[a]
        chain = 2.0 * here - one_bead_ref[a] - other_bead_ref[a]
        total = force_ref[a : a + 1, :] + extra[a] - KAPPA * mass * chain
        velocity = velocity_ref[a] + DT * (total / mass)
        place = here + DT * velocity
        new_velocity_ref[a] = velocity
        new_position_ref[a] = place
        rows.append(place)
    if not last:
        send_rows(rows, species.astype(F32), lists, rest[0], rest[1], wide)


def each(count, body, carry=0):
    for c in range(count // ROWS):
        carry = body(c, carry)
    return carry


def chunk_rows(c, first=0):
    return slice(first + c * ROWS, first + (c + 1) * ROWS)


def own_kernel(
    position_ref,
    species_ref,
    projection_ref,
    shift_ref,
    cols,
    waves,
    turned,
    rows_in,
):
    own = position_ref.shape[2]
    features = projection_ref.shape[2]
    rows_in[...] = jnp.zeros_like(rows_in)
    for a in range(3):
        rows_in[a : a + 1, :] = position_ref[a]
    rows_in[3:4, :] = species_ref[...].astype(F32)
    cols[...] = rows_in[...].T

    shift_cos, shift_sin = cos_sin(shift_ref[...] * TURN)
    for block in range(features // FB):
        mine = slice(block * FB, (block + 1) * FB)
        base = block * 4 * FB
        wave = [
            [projection_ref[a, s : s + 1, mine] * TURN for a in range(3)] for s in range(2)
        ]
        turn_cos = [shift_cos[s : s + 1, mine] for s in range(2)]
        turn_sin = [shift_sin[s : s + 1, mine] for s in range(2)]

        def own_waves(c, carry):
            rows = chunk_rows(c)
            there = cols[rows, :]
            x, y, z = (jnp.broadcast_to(there[:, a : a + 1], (ROWS, FB)) for a in range(3))
            second = jnp.broadcast_to(there[:, 3:4], (ROWS, FB)) > 0.5
            for s in range(2):
                cos, sin = cos_sin(x * wave[s][0] + y * wave[s][1] + z * wave[s][2])
                at = base + s * 2 * FB
                turned[rows, at : at + FB] = turn_cos[s] * cos + turn_sin[s] * sin
                turned[rows, at + FB : at + 2 * FB] = turn_sin[s] * cos - turn_cos[s] * sin
                if s == 0:
                    cos, sin = jnp.where(second, 0.0, cos), jnp.where(second, 0.0, sin)
                else:
                    cos, sin = jnp.where(second, cos, 0.0), jnp.where(second, sin, 0.0)
                waves[rows, at : at + FB] = cos.astype(BF16)
                waves[rows, at + FB : at + 2 * FB] = sin.astype(BF16)
            return carry

        each(own, own_waves)


def weigh_kernel(
    position_ref,
    near_ref,
    far_ref,
    own_cols,
    projection_ref,
    *rest,
):
    *numbers, ghost_cols, weight, weight_turned, waves, rows_in = rest
    own = position_ref.shape[2]
    sent = near_ref.shape[1]
    features = projection_ref.shape[2]

    rows_in[...] = jnp.zeros_like(rows_in)
    rows_in[0:4, 0:sent] = near_ref[...]
    rows_in[0:4, sent : 2 * sent] = far_ref[...]
    ghost_cols[...] = rows_in[...].T
    here = [position_ref[a] for a in range(3)]

    for k, number_ref in enumerate(numbers):
        first = k * number_ref.shape[0]
        cols, skip = (own_cols, first) if first < own else (ghost_cols, first - own)

        def weigh(c, carry):
            there = cols[chunk_rows(c, skip), :]
            square = 0.0
            for a in range(3):
                d = there[:, a : a + 1] - here[a]
                square = square + d * d
            weight[chunk_rows(c, first), :] = number_ref[chunk_rows(c), :] * jnp.exp(
                square * (-1.0 / (2.0 * WIDTH * WIDTH))
            )
            return carry

        each(number_ref.shape[0], weigh)
    weight_turned[...] = weight[...].T.astype(BF16)

    for block in range(features // FB):
        mine = slice(block * FB, (block + 1) * FB)
        base = block * 4 * FB
        wave = [
            [projection_ref[a, s : s + 1, mine] * TURN for a in range(3)] for s in range(2)
        ]

        def ghost_waves(c, carry):
            rows = chunk_rows(c)
            there = ghost_cols[rows, :]
            x, y, z = (jnp.broadcast_to(there[:, a : a + 1], (ROWS, FB)) for a in range(3))
            second = jnp.broadcast_to(there[:, 3:4], (ROWS, FB)) > 0.5
            px, py, pz = (jnp.where(second, wave[1][a], wave[0][a]) for a in range(3))
            cos, sin = cos_sin(x * px + y * py + z * pz)
            for s in range(2):
                at = base + s * 2 * FB
                for k, part in enumerate((cos, sin)):
                    if s == 0:
                        part = jnp.where(second, 0.0, part)
                    else:
                        part = jnp.where(second, part, 0.0)
                    waves[rows, at + k * FB : at + (k + 1) * FB] = part.astype(BF16)
            return carry

        each(2 * sent, ghost_waves)


def describe_kernel(
    weight_turned,
    own_waves,
    ghost_waves,
    turned,
    sines,
    low,
    sums,
):
    own = weight_turned.shape[0]
    features = low.shape[1]
    for block in range(features // FB):
        mine = slice(block * FB, (block + 1) * FB)
        base = block * 4 * FB
        sums[...] = jnp.dot(
            weight_turned[:, 0:own], own_waves[:, base : base + 4 * FB], preferred_element_type=F32
        ) + jnp.dot(
            weight_turned[:, own:], ghost_waves[:, base : base + 4 * FB], preferred_element_type=F32
        )

        def describe(c, carry):
            rows = chunk_rows(c)
            total = 0.0
            for s in range(2):
                at = base + s * 2 * FB
                tr, ti = turned[rows, at : at + FB], turned[rows, at + FB : at + 2 * FB]
                ur = sums[rows, s * 2 * FB : s * 2 * FB + FB]
                ui = sums[rows, s * 2 * FB + FB : s * 2 * FB + 2 * FB]
                total = total + (tr * ur - ti * ui)
                first = s * features + block * FB
                sines[rows, first : first + FB] = tr * ui + ti * ur
            low[rows, mine] = total.astype(BF16)
            return carry

        each(own, describe)


def weigh_describe_kernel(
    position_ref, near_ref, far_ref, own_cols, projection_ref, own_waves, turned, *rest
):
    *numbers, ghost_cols, weight, ghost_waves, sines, low, rows_in, weight_turned, sums = rest
    weigh_kernel(
        position_ref,
        near_ref,
        far_ref,
        own_cols,
        projection_ref,
        *numbers,
        ghost_cols,
        weight,
        weight_turned,
        ghost_waves,
        rows_in,
    )
    describe_kernel(weight_turned, own_waves, ghost_waves, turned, sines, low, sums)


def fold(value):
    total = value[:, 0:LANES]
    for k in range(1, value.shape[1] // LANES):
        total = total + value[:, k * LANES : (k + 1) * LANES]
    return total


def pull_rows(first, cols, waves, weight, spread, projection_ref, here, parts, back, product):
    count = cols.shape[0]
    features = projection_ref.shape[2]
    held = weight[first : first + count, :].astype(BF16)
    for block in range(features // FB):
        mine = slice(block * FB, (block + 1) * FB)
        base = block * 4 * FB
        raw = [[projection_ref[a, s : s + 1, mine] for a in range(3)] for s in range(2)]
        back[...] = jnp.dot(held, spread[:, base : base + 4 * FB], preferred_element_type=F32)

        def pull(c, carry):
            rows = chunk_rows(c)
            second = jnp.broadcast_to(cols[rows, 3:4], (ROWS, FB)) > 0.5
            total = 0.0
            for s in range(2):
                at = base + s * 2 * FB
                er = waves[rows, at : at + FB].astype(F32)
                ei = waves[rows, at + FB : at + 2 * FB].astype(F32)
                vr = back[rows, s * 2 * FB : s * 2 * FB + FB]
                vi = back[rows, s * 2 * FB + FB : s * 2 * FB + 2 * FB]
                total = total + (ei * vr - er * vi)
            for a in range(3):
                coeff = jnp.where(second, raw[1][a], raw[0][a])
                parts[a, rows, :] = parts[a, rows, :] + fold(total * coeff)
            return carry

        each(count, pull)

    product[...] = lax.dot_general(
        waves[...], spread[...], (((1,), (1,)), ((), ())), preferred_element_type=F32
    )

    def along(c, carry):
        rows = chunk_rows(c)
        there = cols[rows, :]
        z = weight[chunk_rows(c, first), :] * product[rows, :] * (1.0 / (WIDTH * WIDTH))
        out = []
        for a in range(3):
            pull_a = z * (there[:, a : a + 1] - here[a])
            parts[a, rows, :] = parts[a, rows, :] + fold(pull_a)
            total = pull_a[0:8]
            for k in range(1, ROWS // 8):
                total = total + pull_a[8 * k : 8 * k + 8]
            out.append(carry[a] + total)
        return tuple(out)

    start = tuple(jnp.zeros((8, here[0].shape[1]), F32) for _ in range(3))
    return each(count, along, carry=start)


def ghost_force_kernel(
    low,
    half_ref,
    other_ref,
    own_cols,
    turned,
    weight,
    waves,
    cols,
    position_ref,
    projection_ref,
    grad,
    spread,
    centre_ref,
    near_ref,
    far_ref,
    back,
    product,
    parts,
):
    own, features = grad.shape
    sent = near_ref.shape[1]
    here = [position_ref[a] for a in range(3)]
    mine_is = core_of().astype(F32)
    grad[...] = jnp.where(
        own_cols[:, 3:4] == mine_is,
        jnp.dot(low[...], half_ref[...], preferred_element_type=F32),
        jnp.dot(low[...], other_ref[...], preferred_element_type=F32),
    )
    for block in range(features // FB):
        mine = slice(block * FB, (block + 1) * FB)
        base = block * 4 * FB

        def spread_out(c, carry):
            rows = chunk_rows(c)
            g = grad[rows, mine]
            for s in range(2):
                at = base + s * 2 * FB
                spread[rows, at : at + FB] = (g * turned[rows, at : at + FB]).astype(BF16)
                spread[rows, at + FB : at + 2 * FB] = (
                    -g * turned[rows, at + FB : at + 2 * FB]
                ).astype(BF16)
            return carry

        each(own, spread_out)

    parts[...] = jnp.zeros_like(parts)
    centre = pull_rows(
        own, cols, waves, weight, spread, projection_ref, here, parts, back, product
    )
    for a in range(3):
        row = jnp.sum(parts[a].T, axis=0, keepdims=True)
        centre_ref[a : a + 1, :] = jnp.sum(centre[a], axis=0, keepdims=True)
        near_ref[a : a + 1, :] = row[:, 0:sent]
        far_ref[a : a + 1, :] = row[:, sent:]


def own_force_kernel(
    grad,
    spread,
    sines,
    waves,
    weight,
    cols,
    position_ref,
    centre_ref,
    projection_ref,
    force_ref,
    back,
    product,
    parts,
):
    own, features = grad.shape
    here = [position_ref[a] for a in range(3)]
    raw = [[projection_ref[a, s : s + 1, :] for a in range(3)] for s in range(2)]

    def turn(c, carry):
        rows = chunk_rows(c)
        g = grad[rows, :]
        t0 = g * sines[rows, 0:features]
        t1 = g * sines[rows, features : 2 * features]
        for a in range(3):
            parts[a, rows, :] = -fold(t0 * raw[0][a] + t1 * raw[1][a])
        return carry

    each(own, turn)
    centre = pull_rows(
        0, cols, waves, weight, spread, projection_ref, here, parts, back, product
    )
    for a in range(3):
        row = jnp.sum(parts[a].T, axis=0, keepdims=True)
        force_ref[a : a + 1, :] = (
            row - jnp.sum(centre[a], axis=0, keepdims=True) - centre_ref[a : a + 1, :]
        )


def routed(block, axis, source):
    return lax.ppermute(block, axis, [(source(i), i) for i in range(lax.axis_size(axis))])


def near_pair(block):
    return routed(block, "dom", lambda i: i ^ 1)


def far_pair(block):
    return routed(block, "dom", lambda i: (i - 1 + i % 2 * 2) % lax.axis_size("dom"))


def across(block):
    beads = lax.axis_size("bead")
    route = [(i ^ (2 * beads + 4), i) for i in range(beads * lax.axis_size("dom"))]
    return lax.ppermute(block, ("dom", "bead"), route)


def even_bead(block):
    return routed(block, "bead", lambda i: i ^ 1)


def odd_bead(block):
    return routed(block, "bead", lambda i: (i - 1 + i % 2 * 2) % lax.axis_size("bead"))


def after(value, *others):
    return lax.optimization_barrier((value, others))[0]


def matrix_part(points, point_weights):
    dom = lax.axis_index("dom")
    which, height = dom % 2, points.shape[2] // 4
    p = lax.dynamic_index_in_dim(points, which, 0, keepdims=False).astype(F32)
    w = lax.dynamic_index_in_dim(point_weights, which, 0, keepdims=False).astype(F32)
    left = lax.dynamic_slice_in_dim(p, dom // 4 * height, height, axis=1)
    return lax.dot_general(
        left * (2.0 * w)[:, None],
        p,
        (((0,), (0,)), ((), ())),
        precision=lax.Precision.HIGHEST,
        preferred_element_type=F32,
    )


def add_kernel(part_ref, other_ref, *outs):
    total = part_ref[...] + other_ref[...].astype(F32)
    for out in outs:
        out[...] = total.astype(out.dtype)


def block_at(k):
    width = 128
    return pl.ds(pl.multiple_of(k % 4 * width, width), width)


def cut_kernel(part_ref, *outs):
    height = lax.axis_index("dom") // 4
    for j in range(3):
        block = part_ref[:, block_at(height + j)]
        for out in outs:
            out[:, j * LANES : (j + 1) * LANES] = block.astype(out.dtype)


def ring_kernel(*refs):
    *pieces, out_ref = refs
    height = lax.axis_index("dom") // 4
    for k, piece in enumerate(pieces):
        row = height + 4 - k
        for j in range(3):
            out_ref[block_at(row), block_at(row + j)] = piece[:, j * LANES : (j + 1) * LANES]
        turned = piece[:, LANES : 2 * LANES].astype(F32).T.astype(BF16)
        out_ref[block_at(row + 1), block_at(row)] = turned


def shards(
    positions,
    velocities,
    species,
    neighbours,
    neighbour_count,
    send_lists,
    projection,
    phase_shift,
    points,
    point_weights,
):
    own, sent = positions.shape[2], send_lists.shape[1]
    ghosts = 2 * sent
    everyone = own + ghosts
    features = points.shape[2]
    shape = jax.ShapeDtypeStruct
    species = species.reshape(1, own)
    position, velocity = positions.transpose(1, 0, 2), velocities.transpose(1, 0, 2)
    projection = projection.transpose(1, 0, 2)
    sends = (shape((4, sent), F32),) * 2
    wide = pltpu.VMEM((LANES, own), F32)
    slab = (features // 4, features // 4 * 3)
    counts = neighbour_count.reshape(1, own)

    def count(part, neighbours):
        return call(
            functools.partial(count_kernel, part),
            shape((ghosts, own), F32),
            [pltpu.VMEM((NEIGH, own), F32)],
        )(neighbours, counts)

    own_call = call(
        own_kernel,
        (
            shape((own, LANES), F32),
            shape((own, 4 * features), BF16),
            shape((own, 4 * features), F32),
        ),
        [wide],
        LIMIT,
    )
    weigh_call = call(
        weigh_kernel,
        (
            shape((ghosts, LANES), F32),
            shape((everyone, own), F32),
            shape((own, everyone), BF16),
            shape((ghosts, 4 * features), BF16),
        ),
        [pltpu.VMEM((LANES, ghosts), F32)],
        LIMIT,
    )
    describe_call = call(
        describe_kernel,
        (shape((own, 2 * features), F32), shape((own, features), BF16)),
        [pltpu.VMEM((own, 4 * FB), F32)],
        LIMIT,
    )
    weigh_describe_call = call(
        weigh_describe_kernel,
        (
            shape((ghosts, LANES), F32),
            shape((everyone, own), F32),
            shape((ghosts, 4 * features), BF16),
            shape((own, 2 * features), F32),
            shape((own, features), BF16),
        ),
        [
            pltpu.VMEM((LANES, ghosts), F32),
            pltpu.VMEM((own, everyone), BF16),
            pltpu.VMEM((own, 4 * FB), F32),
        ],
        LIMIT,
    )
    ghost_force_call = call(
        ghost_force_kernel,
        (
            shape((own, features), F32),
            shape((own, 4 * features), BF16),
            shape((3, own), F32),
            shape((3, sent), F32),
            shape((3, sent), F32),
        ),
        [
            pltpu.VMEM((ghosts, 4 * FB), F32),
            pltpu.VMEM((ghosts, own), F32),
            pltpu.VMEM((3, ghosts, LANES), F32),
        ],
        LIMIT,
    )
    own_force_call = call(
        own_force_kernel,
        shape((3, own), F32),
        [
            pltpu.VMEM((own, 4 * FB), F32),
            pltpu.VMEM((own, own), F32),
            pltpu.VMEM((3, own, LANES), F32),
        ],
        LIMIT,
    )

    to_near, to_far = call(first_kernel, sends, [wide])(position, species, send_lists)
    part, sent_part = call(cut_kernel, (shape(slab, F32), shape(slab, BF16)))(
        matrix_part(points, point_weights)
    )
    for step in range(STEPS):
        last = step == STEPS - 1
        if step == 0:
            other = across(sent_part)
            to_far, to_near = after(to_far, sent_part), after(to_near, sent_part)
        from_far = far_pair(to_far)
        from_near = near_pair(to_near)
        if step == 0:
            number = [count(k, neighbours) for k in range(2)]
            part, held = call(add_kernel, (shape(slab, F32), shape(slab, BF16)))(
                part, after(other, from_far, from_near, *number)
            )
            other = routed(held, "bead", lambda i: i ^ 1)
        start = after(position, held) if step == 0 else position
        cols, waves, turned = own_call(start, species, projection, phase_shift)
        if step == 0:
            part, held = call(add_kernel, (shape(slab, F32), shape(slab, BF16)))(
                part, after(other, cols)
            )
            other = routed(held, "bead", lambda i: i ^ 3)
            number.append(count(2, after(neighbours, held)))
            state = weigh_call(
                after(position, held), from_near, from_far, cols, projection, *number
            )
            ghost_cols, weight, weight_turned, ghost_waves = state
            held = call(add_kernel, (shape(slab, BF16),))(part, after(other, *state))[0]
            pieces = [held] + [routed(held, "dom", lambda i: (i - 4 * k) % 16) for k in (1, 2, 3)]
            one_bead = even_bead(after(position, held))
            sines, low = describe_call(after(weight_turned, held), waves, ghost_waves, turned)
            half = call(ring_kernel, shape((features, features), BF16))(
                pieces[0], *[after(piece, low, one_bead) for piece in pieces[1:]]
            )
            other_half = near_pair(half)
            other_bead = odd_bead(after(position, half))
        else:
            one_bead = even_bead(after(position, cols, from_far, from_near))
            ghost_cols, weight, ghost_waves, sines, low = weigh_describe_call(
                position, from_near, from_far, cols, projection, waves, turned, *number
            )
            other_bead = odd_bead(after(position, low))
        grad, spread, centre, near_force, far_force = ghost_force_call(
            low,
            half,
            other_half,
            cols,
            turned,
            weight,
            ghost_waves,
            ghost_cols,
            position,
            projection,
        )
        far_back = far_pair(far_force)
        near_back = near_pair(near_force)
        force = own_force_call(
            grad, spread, sines, waves, weight, cols, position, centre, projection
        )
        moved = shape(position.shape, F32)
        position, velocity, *rest = call(
            functools.partial(update_kernel, last),
            (moved, moved) + (() if last else sends),
            [pltpu.VMEM((LANES, sent), F32), wide],
        )(
            force,
            near_back,
            far_back,
            send_lists,
            position,
            velocity,
            other_bead,
            one_bead,
            species,
        )
        if not last:
            to_near, to_far = rest
    return (position.transpose(1, 0, 2), velocity.transpose(1, 0, 2))


def solution(mesh):
    placed = (
        P("bead", None, "dom"),
        P("bead", None, "dom"),
        P("dom"),
        P(None, "dom"),
        P("dom"),
        P(None, "dom"),
        P(),
        P(),
        P(None, "bead", None),
        P(None, "bead"),
    )
    return jax.shard_map(
        shards,
        mesh=mesh,
        in_specs=placed,
        out_specs=(P("bead", None, "dom"), P("bead", None, "dom")),
        check_vma=False,
    )
```
